512 devices in a mesh: row: 32 (over y_hi, z, core), col: 16 (over x, y_lo).
Axes of the slice: x: 4, y: 8 (y_hi: 2, y_lo: 4; y = y_hi * 4 + y_lo), z: 8, core: 2. Of those that a mesh axis runs over, the one named last changes fastest.
Arguments:
- left_features: bfloat16 [128, 128, 256], P('row', 'col'), may hold values from -6 to 6
- right_features: bfloat16 [128, 128, 256], P('col', 'row'), may hold values from -6 to 6
- flow_offsets: int32 [2, 128, 128], P(None, 'row'), may hold values from -64 to 63
- look_cotangent: bfloat16 [128, 128, 324], P('row', 'col'), may hold values from -6 to 6
- hidden_state: bfloat16 [128, 128, 128], P('row', 'col'), may hold values from -0.8984375 to 0.8984375
- context: bfloat16 [128, 128, 128], P('row', 'col'), may hold values from -6 to 6
- motion_weight: float32 [324, 256], replicated, may hold values from -0.3125 to 0.3125
- row_gates: bfloat16 [5, 512, 256], replicated, may hold values from -0.125 to 0.125
- row_candidate: bfloat16 [5, 512, 128], replicated, may hold values from -0.125 to 0.125
- column_gates: bfloat16 [5, 512, 256], replicated, may hold values from -0.125 to 0.125
- column_candidate: bfloat16 [5, 512, 128], replicated, may hold values from -0.125 to 0.125
Outputs:
- new_hidden: float32 [128, 128, 128], P('row', 'col')
- grad_left: float32 [128, 128, 256], P('row', 'col')
- grad_right: float32 [128, 128, 256], P('col', 'row')
The draws below stay inside these ranges and needn't reach their ends.
All inputs are finite; a program needn't handle non-finite values.
Results may differ from the reference program's by a relative error of at most 0.0029.
Values may be sent and summed in bfloat16 or wider, within the bound.
No kernel may reach another device: no remote copies, remote signals or barrier semaphores. Data moves between devices by JAX's collectives and lax.ppermute only.
A program may use at most 64 MiB of HBM per device.

```python
import jax
import jax.numpy as jnp
from jax import lax

C = 256
HD = 128
CTX = 128
MOT = 256
LEVELS = 4
RADIUS = 4
KS = 5
W = 128
H = 128
LOOK = 324


def set_ends(drawn, own_key, smallest, largest):
    longest = drawn.shape.index(max(drawn.shape))
    spots = []
    for shift in (0, 1):
        where = [jax.random.randint(jax.random.fold_in(own_key, axis), (), 0, length) for axis, length in enumerate(drawn.shape)]
        where[longest] = (where[longest] + shift) % drawn.shape[longest]
        spots.append(tuple(where))
    return drawn.at[spots[0]].set(smallest).at[spots[1]].set(largest)


def block_scale(rng, extent, pieces, smallest, high):
    factor_of = 1.0
    for dim, parts in pieces:
        heights = jax.random.uniform(jax.random.fold_in(jax.random.fold_in(rng, 6), dim), (parts,), jnp.float32, smallest / len(pieces), high / len(pieces))
        factor_of = factor_of * jnp.repeat(jnp.exp(heights), extent[dim] // parts).reshape((-1,) + (1,) * (len(extent) - 1 - dim))
    return factor_of


def normal_values(own_key, extent, scale, bound, shards=(), held_as=jnp.bfloat16):
    result = jax.random.normal(own_key, extent, jnp.float32) * scale
    if len(shards) > 0:
        result = block_scale(own_key, extent, shards, -0.22, 0.18) * result
    return jnp.clip(result, min=-bound, max=bound).astype(held_as)


def setup_inputs(seed: int = 0) -> dict:
    splits = jax.random.split(jax.random.key(seed), 12)
    left_features = normal_values(splits[0], (H, W, C), 1.0, 6.0, ((0, 32), (1, 16)))
    right_features = normal_values(splits[1], (H, W, C), 1.0, 6.0, ((0, 16), (1, 32)))
    flow_offsets = set_ends(jax.random.randint(splits[2], (2, H, W), -(H // 2), H // 2), jax.random.fold_in(splits[2], 1), -(H // 2), (H // 2) - 1).astype(jnp.int32)
    look_cotangent = normal_values(splits[3], (H, W, LOOK), 1.0, 6.0, ((0, 32), (1, 16)))
    hidden_state = jnp.clip(jax.random.uniform(splits[4], (H, W, HD), jnp.float32, -0.8984375, 0.8984375) * block_scale(splits[4], (H, W, HD), ((0, 32), (1, 16)), -0.4, 0.0), -0.8984375, 0.8984375).astype(jnp.bfloat16)
    context = normal_values(splits[5], (H, W, CTX), 1.0, 6.0, ((0, 32), (1, 16)))
    motion_weight = normal_values(splits[6], (LOOK, MOT), LOOK ** -0.5, 0.3125, (), jnp.float32)
    row_gates = normal_values(splits[7], (KS, HD + MOT + CTX, 2 * HD), (KS * (HD + MOT + CTX)) ** -0.5, 0.125)
    row_candidate = normal_values(splits[8], (KS, HD + MOT + CTX, HD), (KS * (HD + MOT + CTX)) ** -0.5, 0.125)
    column_gates = normal_values(splits[9], (KS, HD + MOT + CTX, 2 * HD), (KS * (HD + MOT + CTX)) ** -0.5, 0.125)
    column_candidate = normal_values(splits[10], (KS, HD + MOT + CTX, HD), (KS * (HD + MOT + CTX)) ** -0.5, 0.125)
    return dict(left_features=left_features, right_features=right_features, flow_offsets=flow_offsets, look_cotangent=look_cotangent, hidden_state=hidden_state, context=context, motion_weight=motion_weight, row_gates=row_gates, row_candidate=row_candidate, column_gates=column_gates, column_candidate=column_candidate)


def window_index(center_row, center_col, factor, level_first, level_rows, level_cols):
    offsets = jnp.arange(2 * RADIUS + 1, dtype=jnp.int32) - RADIUS
    rows_at = (jnp.floor_divide(center_row, factor) - level_first)[:, None, None] + offsets[None, :, None]
    cols_at = jnp.floor_divide(center_col, factor)[:, None, None] + offsets[None, None, :]
    inside = (rows_at >= 0) & (rows_at < level_rows) & (cols_at >= 0) & (cols_at < level_cols)
    flat_index = jnp.clip(rows_at, 0, level_rows - 1) * level_cols + jnp.clip(cols_at, 0, level_cols - 1)
    pixel_count = center_row.shape[0]
    return flat_index.reshape(pixel_count, -1).astype(jnp.int32), inside.reshape(pixel_count, -1)


def look_up(volume, center_row, center_col, first_row, rows_here, cols_here):
    pixel_count = volume.shape[0]
    current = volume.reshape(pixel_count, rows_here, cols_here)
    found_list = []
    for level_index in range(LEVELS):
        factor = 2 ** level_index
        if level_index > 0:
            shape_now = current.shape
            current = current.reshape(pixel_count, shape_now[1] // 2, 2, shape_now[2] // 2, 2).mean(axis=(2, 4))
        flat_index, inside = window_index(center_row, center_col, factor, first_row // factor, rows_here // factor, cols_here // factor)
        picked = jnp.take_along_axis(current.reshape(pixel_count, -1), flat_index, axis=1)
        found_list.append(jnp.where(inside, picked, jnp.float32(0.0)))
    return jnp.concatenate(found_list, axis=1)


def spread_back(cotangent, center_row, center_col, first_row, rows_here, cols_here):
    pixel_count = cotangent.shape[0]
    window_area = (2 * RADIUS + 1) ** 2
    summed = jnp.zeros((pixel_count, rows_here, cols_here), jnp.float32)
    for level_index in range(LEVELS):
        factor = 2 ** level_index
        level_rows = rows_here // factor
        level_cols = cols_here // factor
        flat_index, inside = window_index(center_row, center_col, factor, first_row // factor, level_rows, level_cols)
        values = jnp.where(inside, cotangent[:, level_index * window_area:(level_index + 1) * window_area].astype(jnp.float32), jnp.float32(0.0))

        def add_level(index_row, value_row):
            return jnp.zeros((level_rows * level_cols,), jnp.float32).at[index_row].add(value_row)

        level_grid = jax.vmap(add_level)(flat_index, values) / (factor * factor)
        expanded = jnp.broadcast_to(level_grid.reshape(pixel_count, level_rows, 1, level_cols, 1), (pixel_count, level_rows, factor, level_cols, factor))
        summed = summed + expanded.reshape(pixel_count, rows_here, cols_here)
    return summed.reshape(pixel_count, rows_here * cols_here)


def taps(source, weight, axis_index, length):
    summed = None
    for tap_index in range(weight.shape[0]):
        window_slice = lax.slice_in_dim(source, tap_index, tap_index + length, axis=axis_index)
        product = jnp.einsum("abi,io->abo", window_slice, weight[tap_index], preferred_element_type=jnp.float32)
        summed = product if summed is None else summed + product
    return summed


def gru_pass(prior_state, inputs, gates_weight, candidate_weight, axis_index, length):
    hidden_size = prior_state.shape[-1]
    joined = jnp.concatenate([prior_state, inputs], axis=-1)
    gate_pair = jax.nn.sigmoid(taps(joined, gates_weight, axis_index, length + 4))
    update = gate_pair[..., :hidden_size]
    reset_gate = gate_pair[..., hidden_size:]
    inner_state = lax.slice_in_dim(prior_state, 2, length + 6, axis=axis_index).astype(jnp.float32)
    reset_state = (reset_gate * inner_state).astype(jnp.bfloat16)
    inner_inputs = lax.slice_in_dim(inputs, 2, length + 6, axis=axis_index)
    candidate = jnp.tanh(taps(jnp.concatenate([reset_state, inner_inputs], axis=-1), candidate_weight, axis_index, length))
    center_state = lax.slice_in_dim(prior_state, 4, length + 4, axis=axis_index).astype(jnp.float32)
    center_update = lax.slice_in_dim(update, 2, length + 2, axis=axis_index)
    return (1.0 - center_update) * center_state + center_update * candidate


def reference(left_features, right_features, flow_offsets, look_cotangent, hidden_state, context, motion_weight, row_gates, row_candidate, column_gates, column_candidate):
    height, width, channels = left_features.shape
    factor = channels ** -0.5
    right_flat = right_features.reshape(height * width, channels)
    col_ids = jnp.arange(width, dtype=jnp.int32)

    def one_row(grad_right, inputs_row):
        row_id, left_row, cot_row, offset_row = inputs_row
        center_row = row_id + offset_row[0]
        center_col = col_ids + offset_row[1]
        volume = lax.dot_general(left_row, right_flat, (((1,), (1,)), ((), ())), preferred_element_type=jnp.float32) * factor
        looked = look_up(volume, center_row, center_col, 0, height, width)
        spread = spread_back(cot_row, center_row, center_col, 0, height, width).astype(jnp.bfloat16)
        grad_left_row = jnp.dot(spread, right_flat, preferred_element_type=jnp.float32) * factor
        grad_right = grad_right + lax.dot_general(spread, left_row, (((0,), (0,)), ((), ())), preferred_element_type=jnp.float32) * factor
        return grad_right, (looked, grad_left_row)

    row_range = jnp.arange(height, dtype=jnp.int32)
    offsets_rows = jnp.transpose(flow_offsets, (1, 0, 2))
    grad_right, (looked, grad_left) = lax.scan(one_row, jnp.zeros((height * width, channels), jnp.float32), (row_range, left_features, look_cotangent, offsets_rows))
    motion = jax.nn.relu(jnp.dot(looked.reshape(height * width, -1), motion_weight, precision=lax.Precision.HIGHEST))
    motion = motion.astype(jnp.bfloat16).reshape(height, width, -1)
    inputs = jnp.concatenate([motion, context], axis=-1)
    state_cols = jnp.pad(hidden_state, ((0, 0), (4, 4), (0, 0)))
    inputs_cols = jnp.pad(inputs, ((0, 0), (4, 4), (0, 0)))
    middle_state = gru_pass(state_cols, inputs_cols, row_gates, row_candidate, 1, width).astype(jnp.bfloat16)
    state_rows = jnp.pad(middle_state, ((4, 4), (0, 0), (0, 0)))
    inputs_rows = jnp.pad(inputs, ((4, 4), (0, 0), (0, 0)))
    new_hidden = gru_pass(state_rows, inputs_rows, column_gates, column_candidate, 0, height)
    return new_hidden, grad_left, grad_right.reshape(height, width, channels)
```

```python
import jax
import jax.numpy as jnp
import numpy as np
from jax import lax
from jax.experimental import pallas as pl
from jax.experimental.pallas import tpu as pltpu
from jax.sharding import PartitionSpec as P

LEVELS = 4
RADIUS = 4
SIDE = 2 * RADIUS + 1
AREA = SIDE * SIDE
LANES = 128
F32 = jnp.float32
BF16 = jnp.bfloat16
I32 = jnp.int32


def iota(shape, dim):
    return lax.broadcasted_iota(I32, shape, dim)


def target_of(row, strip, col):
    return ((row >> 3) << 6) | (strip << 5) | ((row & 7) << 2) | col


def pool_matrix(rows, strips, width):
    count = np.arange(rows * strips * width)
    strip, row, col = count // (rows * width), count // width % rows, count % width
    target = target_of(row, strip, col)
    parts = []
    for level in (1, 2, 3):
        high, wide = rows >> level, max(width >> level, 1)
        cell = (strip * high + (row >> level)) * wide + (col >> level)
        part = np.zeros((strips * high * wide, count.size), np.float32)
        part[cell, target] = 0.25**level
        parts.append(part)
    pooled = np.concatenate(parts, axis=0)
    padded = -(-pooled.shape[0] // LANES) * LANES
    return np.pad(pooled, ((0, padded - pooled.shape[0]), (0, 0))).astype(BF16)


def take(values, index):
    return jnp.take_along_axis(values, index & (LANES - 1), axis=1, mode="promise_in_bounds")


def inside(index, count):
    return (index >= 0) & (index < count)


def pack(cells, tile_cols, channels, lefts):
    width = channels + LEVELS * AREA + 2

    def kernel(left_ref, cot_ref, flow_ref, right_ref, lefts_hbm, right_out, left, wide, sems):
        first_col = lax.axis_index(COL) * tile_cols
        for row in range(right_ref.shape[0]):
            step = right_ref.shape[1]
            wide[row * step : (row + 1) * step, :] = right_ref[row].astype(F32)
        right_out[...] = wide[...].astype(BF16)
        left[:, :channels] = left_ref[...]
        left[:, channels : width - 2] = cot_ref[...]
        chosen = iota((tile_cols, LANES), 1) == first_col + iota((tile_cols, LANES), 0)
        for axis in range(2):
            columns = []
            for row in range(cells // tile_cols):
                values = jnp.broadcast_to(flow_ref[axis, row : row + 1, :].astype(F32), (tile_cols, LANES))
                columns.append(jnp.sum(jnp.where(chosen, values, 0.0), axis=1, keepdims=True))
            column = jnp.concatenate(columns, axis=0).astype(BF16)
            left[:, width - 2 + axis : width - 1 + axis] = column
        copies = [pltpu.make_async_copy(left, lefts_hbm.at[i], sems.at[i]) for i in range(lefts)]
        for copy in copies:
            copy.start()
        for copy in copies:
            copy.wait()

    vmem, hbm = pl.BlockSpec(memory_space=pltpu.VMEM), pl.BlockSpec(memory_space=pltpu.HBM)
    return pl.pallas_call(
        kernel,
        out_shape=(
            jax.ShapeDtypeStruct((lefts, cells, width), BF16),
            jax.ShapeDtypeStruct((cells, channels), BF16),
        ),
        in_specs=[vmem] * 4,
        out_specs=[hbm, vmem],
        scratch_shapes=[
            pltpu.VMEM((cells, width), BF16),
            pltpu.VMEM((cells, channels), F32),
            pltpu.SemaphoreType.DMA((lefts,)),
        ],
        compiler_params=pltpu.CompilerParams(vmem_limit_bytes=60 * 2**20),
        name="pack",
    )


def centers_of(place, given, index, chunk):
    shape = (chunk, LANES)
    pixel = index * chunk + iota(shape, 0)
    core = place[2] ^ (pixel >> 8)
    row = place[0] + ((pixel >> 5) & 7) * 8 + core * 4 + ((pixel >> 3) & 3)
    col = place[1] + (pixel & 7)
    row = row + jnp.broadcast_to(given[:, LEVELS * AREA : LEVELS * AREA + 1], shape).astype(I32)
    col = col + jnp.broadcast_to(given[:, LEVELS * AREA + 1 : LEVELS * AREA + 2], shape).astype(I32)
    return [(row >> level, col >> level) for level in range(LEVELS)]


def spread_out(pixels, channels, targets, chunk, blocks):
    tiles = targets // LANES
    size = targets // blocks
    half = pixels // 2

    def kernel(
        place, own_ref, other_ref, pool_ref, spread_hbm, grad_hbm,
        left, rest, fine, coarse, spread_ref, grad_ref, sems,
    ):
        scale = channels**-0.5
        first = place[3]
        left[:half, :] = own_ref[:, :channels]
        left[half:, :] = other_ref[:, :channels]
        rest[:half, :] = own_ref[:, channels:]
        rest[half:, :] = other_ref[:, channels:]

        def step(index, carry):
            rows = pl.ds(pl.multiple_of(index * chunk, chunk), chunk)
            shape = (chunk, LANES)
            lane = iota(shape, 1)
            given = rest[rows, :].astype(F32)
            centers = centers_of(place, given, index, chunk)
            cots = []
            for level in range(LEVELS):
                part = given[:, level * AREA : (level + 1) * AREA]
                cots.append(jnp.pad(part, ((0, 0), (0, LANES - AREA))))

            def window(level, row, col):
                a, b = row - centers[level][0], col + (first >> level) - centers[level][1]
                valid = (jnp.abs(a) <= RADIUS) & (jnp.abs(b) <= RADIUS)
                return jnp.where(valid, take(cots[level], a * SIDE + b + AREA // 2), 0.0)

            flip = place[4]
            a = ((lane >> 6) << 3) + ((lane >> 2) & 7) - centers[0][0]
            b = ((((lane >> 5) & 1) ^ flip) << 6) + (lane & 3) + first - centers[0][1]
            near_col = jnp.abs(b) <= RADIUS
            entry = a * SIDE + b + AREA // 2
            for tile in range(tiles):
                valid = near_col & (jnp.abs(a + 16 * tile) <= RADIUS)
                picked = take(cots[0], entry + 16 * SIDE * tile)
                fine[rows, tile * LANES : (tile + 1) * LANES] = jnp.where(valid, picked, 0.0)
            for tile in range(2):
                cell = window(1, lane >> 1, ((tile ^ flip) << 5) + (lane & 1))
                coarse[rows, tile * LANES : (tile + 1) * LANES] = cell.astype(BF16)
            second = window(2, lane & 31, (((lane >> 5) & 1) ^ flip) << 4)
            third = window(3, lane & 15, (((lane >> 4) & 1) ^ flip) << 3)
            cell = jnp.where(lane < 64, second, jnp.where(lane < 96, third, 0.0))
            coarse[rows, 2 * LANES :] = cell.astype(BF16)
            return carry

        lax.fori_loop(0, pixels // chunk, step, 0)

        spread = (fine[...] + jnp.dot(coarse[...], pool_ref[...], preferred_element_type=F32)).astype(BF16)
        spread_ref[...] = spread
        spread_copy = pltpu.make_async_copy(spread_ref, spread_hbm, sems.at[0])
        spread_copy.start()
        grad_ref[...] = (
            lax.dot_general(spread, left[...], (((0,), (0,)), ((), ())), preferred_element_type=F32) * scale
        ).astype(BF16)
        grad_copies = []
        for block in range(blocks):
            owner = ((block & 1) ^ place[4]) * (blocks // 2) + (block >> 1)
            copy = pltpu.make_async_copy(
                grad_ref.at[block * size : (block + 1) * size], grad_hbm.at[owner], sems.at[1 + block]
            )
            copy.start()
            grad_copies.append(copy)
        spread_copy.wait()
        for copy in grad_copies:
            copy.wait()

    vmem, hbm = pl.BlockSpec(memory_space=pltpu.VMEM), pl.BlockSpec(memory_space=pltpu.HBM)
    return pl.pallas_call(
        kernel,
        out_shape=(
            jax.ShapeDtypeStruct((pixels, targets), BF16),
            jax.ShapeDtypeStruct((blocks, size, channels), BF16),
        ),
        in_specs=[pl.BlockSpec(memory_space=pltpu.SMEM)] + [vmem] * 3,
        out_specs=[hbm] * 2,
        scratch_shapes=[
            pltpu.VMEM((pixels, channels), BF16),
            pltpu.VMEM((pixels, LEVELS * AREA + 2), BF16),
            pltpu.VMEM((pixels, targets), F32),
            pltpu.VMEM((pixels, 3 * LANES), BF16),
            pltpu.VMEM((pixels, targets), BF16),
            pltpu.VMEM((targets, channels), BF16),
            pltpu.SemaphoreType.DMA((1 + blocks,)),
        ],
        compiler_params=pltpu.CompilerParams(vmem_limit_bytes=24 * 2**20),
        cost_estimate=pl.CostEstimate(flops=5 * 10**9, bytes_accessed=4 * 10**6, transcendentals=0),
        name="spread_out",
    )


def look_up(pixels, channels, targets, chunk):
    tiles = targets // LANES
    half = pixels // 2

    def kernel(
        place, own_ref, other_ref, right_ref, spread_hbm, pool_ref, motion_ref,
        out_own, out_other, left, rest, vol, looked, looked_low, weight, spread_ref, sem,
    ):
        spread_copy = pltpu.make_async_copy(spread_hbm, spread_ref, sem)
        spread_copy.start()
        scale = channels**-0.5
        first = place[3]
        left[:half, :] = own_ref[:, :channels]
        left[half:, :] = other_ref[:, :channels]
        rest[:half, :] = own_ref[:, channels:]
        rest[half:, :] = other_ref[:, channels:]
        weight[...] = jnp.zeros(weight.shape, F32)
        for level in range(LEVELS):
            weight[level * LANES : level * LANES + AREA, :] = motion_ref[level * AREA : (level + 1) * AREA, :]
        right = right_ref[...]
        contract_last = (((1,), (1,)), ((), ()))
        pooled = jnp.dot(pool_ref[...], right, preferred_element_type=F32)
        high = pooled.astype(BF16)
        low = (pooled - high.astype(F32)).astype(BF16)
        vol[:, :targets] = lax.dot_general(left[...], right, contract_last, preferred_element_type=F32)
        vol[:, targets:] = lax.dot_general(
            left[...], high, contract_last, preferred_element_type=F32
        ) + lax.dot_general(left[...], low, contract_last, preferred_element_type=F32)

        def step(index, carry):
            rows = pl.ds(pl.multiple_of(index * chunk, chunk), chunk)
            shape = (chunk, LANES)
            lane = iota(shape, 1)
            a_of = lane // SIDE
            b_of = lane - a_of * SIDE - RADIUS
            a_of = a_of - RADIUS
            in_window = lane < AREA
            centers = centers_of(place, rest[rows, :].astype(F32), index, chunk)
            for level in range(LEVELS):
                height, apart, width = LANES >> level, 64 >> level, max(4 >> level, 1)
                row = centers[level][0] + a_of
                col = centers[level][1] + b_of - (first >> level)
                within = col & (apart - 1)
                valid = inside(row, height) & inside(col, 2 * apart) & (within < width) & in_window
                strip = ((col >> (6 - level)) & 1) ^ place[4]
                start, count = ((0, tiles), (tiles, 2), (tiles + 2, 1), (tiles + 2, 1))[level]
                if level == 0:
                    cell = target_of(row, strip, within)
                else:
                    cell = (strip * height + row) * width + within + (64 if level == 3 else 0)
                which = jnp.where(valid, cell >> 7, -1)
                found = jnp.zeros(shape, F32)
                for tile in range(count):
                    at = (start + tile) * LANES
                    picked = take(vol[rows, at : at + LANES], cell)
                    found = jnp.where(which == tile, picked, found)
                found = found * scale
                upper = found.astype(BF16)
                looked[rows, level * LANES : (level + 1) * LANES] = upper
                looked_low[rows, level * LANES : (level + 1) * LANES] = (found - upper.astype(F32)).astype(BF16)
            return carry

        lax.fori_loop(0, pixels // chunk, step, 0)

        weight_high = weight[...].astype(BF16)
        weight_low = (weight[...] - weight_high.astype(F32)).astype(BF16)
        motion = jnp.dot(looked[...], weight_high, preferred_element_type=F32)
        motion = motion + jnp.dot(looked[...], weight_low, preferred_element_type=F32)
        motion = motion + jnp.dot(looked_low[...], weight_high, preferred_element_type=F32)
        spread_copy.wait()
        grad_left = jnp.dot(spread_ref[...], right, preferred_element_type=F32) * scale
        out_own[:, :channels] = motion[:half]
        out_own[:, channels:] = grad_left[:half]
        out_other[:, :channels] = motion[half:].astype(BF16)
        out_other[:, channels:] = grad_left[half:].astype(BF16)

    vmem, hbm = pl.BlockSpec(memory_space=pltpu.VMEM), pl.BlockSpec(memory_space=pltpu.HBM)
    return pl.pallas_call(
        kernel,
        out_shape=(
            jax.ShapeDtypeStruct((half, 2 * channels), F32),
            jax.ShapeDtypeStruct((half, 2 * channels), BF16),
        ),
        in_specs=[pl.BlockSpec(memory_space=pltpu.SMEM)] + [vmem] * 3 + [hbm] + [vmem] * 2,
        out_specs=[vmem] * 2,
        scratch_shapes=[
            pltpu.VMEM((pixels, channels), BF16),
            pltpu.VMEM((pixels, LEVELS * AREA + 2), BF16),
            pltpu.VMEM((pixels, targets + 3 * LANES), F32),
            pltpu.VMEM((pixels, LEVELS * LANES), BF16),
            pltpu.VMEM((pixels, LEVELS * LANES), BF16),
            pltpu.VMEM((LEVELS * LANES, channels), F32),
            pltpu.VMEM((pixels, targets), BF16),
            pltpu.SemaphoreType.DMA,
        ],
        compiler_params=pltpu.CompilerParams(vmem_limit_bytes=24 * 2**20),
        cost_estimate=pl.CostEstimate(flops=6 * 10**9, bytes_accessed=4 * 10**6, transcendentals=0),
        name="look_up",
    )


def add_up(parts, cells, channels, hidden_size):
    def kernel(parts_ref, hidden_ref, context_ref, joined_ref, grad_ref):
        total = parts_ref[0].astype(F32)
        for part in range(1, parts):
            total = total + parts_ref[part].astype(F32)
        joined_ref[:, :hidden_size] = hidden_ref[...]
        joined_ref[:, hidden_size : hidden_size + channels] = jnp.maximum(total[:, :channels], 0.0).astype(BF16)
        joined_ref[:, hidden_size + channels :] = context_ref[...]
        grad_ref[...] = total[:, channels:]

    vmem, hbm = pl.BlockSpec(memory_space=pltpu.VMEM), pl.BlockSpec(memory_space=pltpu.HBM)
    return pl.pallas_call(
        kernel,
        out_shape=(
            jax.ShapeDtypeStruct((cells, 2 * channels), BF16),
            jax.ShapeDtypeStruct((cells, channels), F32),
        ),
        in_specs=[vmem] * 3,
        out_specs=[vmem] * 2,
        compiler_params=pltpu.CompilerParams(vmem_limit_bytes=16 * 2**20),
        name="add_up",
    )


def sum_parts(parts, rows, cols, channels):
    def kernel(parts_ref, out_ref):
        total = parts_ref[0].astype(F32)
        for part in range(1, parts):
            total = total + parts_ref[part].astype(F32)
        for row in range(rows):
            out_ref[row] = total[row * cols : (row + 1) * cols]

    vmem = pl.BlockSpec(memory_space=pltpu.VMEM)
    return pl.pallas_call(
        kernel,
        out_shape=jax.ShapeDtypeStruct((rows, cols, channels), F32),
        in_specs=[vmem],
        out_specs=vmem,
        compiler_params=pltpu.CompilerParams(vmem_limit_bytes=16 * 2**20),
        name="sum_parts",
    )


def warm(*weights):
    def kernel(*refs):
        total = refs[0][0, :16, :LANES]
        for ref in refs[1:-1]:
            total = total + ref[0, :16, :LANES]
        refs[-1][...] = total

    vmem = pl.BlockSpec(memory_space=pltpu.VMEM)
    return pl.pallas_call(
        kernel,
        out_shape=jax.ShapeDtypeStruct((16, LANES), BF16),
        in_specs=[vmem] * len(weights),
        out_specs=vmem,
        compiler_params=pltpu.CompilerParams(vmem_limit_bytes=24 * 2**20),
        cost_estimate=pl.CostEstimate(flops=2 * 10**9, bytes_accessed=4 * 10**6, transcendentals=0),
        name="warm",
    )(*weights)


def gru(tile_rows, tile_cols, hidden_size, taps):
    high, wide = tile_rows + 8, tile_cols + 8

    def sigmoid(x):
        return 1.0 / (1.0 + jnp.exp(-x))

    def kernel(cells_ref, rg_ref, rc_ref, cg_ref, cc_ref, warm_ref, out_ref):
        flat = high * wide
        hidden_bf = cells_ref[:, :, :hidden_size].reshape(flat, hidden_size)
        inputs = cells_ref[:, :, hidden_size:].reshape(flat, -1)
        hidden = hidden_bf.astype(F32)

        def conv_x(source, weight_ref):
            total = None
            for tap in range(taps):
                product = jnp.dot(source, weight_ref[tap], preferred_element_type=F32)
                shift = (2 - tap) % flat
                if shift:
                    product = pltpu.roll(product, shift, 0)
                total = product if total is None else total + product
            return total

        gates = sigmoid(conv_x(jnp.concatenate([hidden_bf, inputs], axis=-1), rg_ref))
        update, reset = gates[:, :hidden_size], gates[:, hidden_size:]
        reset_state = (reset * hidden).astype(BF16)
        candidate = jnp.tanh(conv_x(jnp.concatenate([reset_state, inputs], axis=-1), rc_ref))
        middle = (1.0 - update) * hidden + update * candidate

        def own_columns(values):
            moved = pltpu.roll(values, flat - 4, 0).reshape(high, wide, -1)
            return moved[:, :tile_cols].reshape(high * tile_cols, -1)

        middle_bf = own_columns(middle).astype(BF16)
        inputs = own_columns(inputs.astype(F32)).astype(BF16)
        middle = middle_bf.astype(F32)

        def conv_y(source, weight_ref, count):
            total = None
            for tap in range(taps):
                product = jnp.dot(source, weight_ref[tap], preferred_element_type=F32)
                part = product[tap * tile_cols : (tap + count) * tile_cols]
                total = part if total is None else total + part
            return total

        gates = sigmoid(conv_y(jnp.concatenate([middle_bf, inputs], axis=-1), cg_ref, high - 4))
        reset = gates[:, hidden_size:]
        update = gates[2 * tile_cols : (2 + tile_rows) * tile_cols, :hidden_size]
        reset_state = (reset * middle[2 * tile_cols : (high - 2) * tile_cols]).astype(F32)
        edge = jnp.zeros((2 * tile_cols, hidden_size), F32)
        reset_state = jnp.concatenate([edge, reset_state, edge], axis=0).astype(BF16)
        joined = jnp.concatenate([reset_state, inputs], axis=-1)
        total = None
        for tap in range(taps):
            product = jnp.dot(joined, cc_ref[tap], preferred_element_type=F32)
            part = product[(tap + 2) * tile_cols : (tap + 2 + tile_rows) * tile_cols]
            total = part if total is None else total + part
        candidate = jnp.tanh(total)
        center = middle[4 * tile_cols : (4 + tile_rows) * tile_cols]
        out_ref[...] = (1.0 - update) * center + update * candidate

    return pl.pallas_call(
        kernel,
        out_shape=jax.ShapeDtypeStruct((tile_rows * tile_cols, hidden_size), F32),
        in_specs=[pl.BlockSpec(memory_space=pltpu.VMEM)] * 6,
        out_specs=pl.BlockSpec(memory_space=pltpu.VMEM),
        compiler_params=pltpu.CompilerParams(vmem_limit_bytes=24 * 2**20),
        cost_estimate=pl.CostEstimate(flops=10**9, bytes_accessed=5 * 10**6, transcendentals=10**5),
        name="gru",
    )


def with_halo(cells, axis, dim, width):
    count = lax.axis_size(axis)
    ends = count - 1
    head = lax.slice_in_dim(cells, 0, width, axis=dim)
    tail = lax.slice_in_dim(cells, cells.shape[dim] - width, cells.shape[dim], axis=dim)
    return jnp.concatenate(
        [
            lax.ppermute(tail, axis, [(i, (i + 1) % count) for i in range(ends)]),
            cells,
            lax.ppermute(head, axis, [((i + 1) % count, i) for i in range(ends)]),
        ],
        axis=dim,
    )


def swap(block, axis, bit):
    return lax.ppermute(block, axis, [(i, i ^ bit) for i in range(lax.axis_size(axis))])


ROW = ("yh", "z", "core")
COL = ("x", "yl")
SPREAD = ("yh", "x", "yl")


def shards(
    left_features,
    right_features,
    flow_offsets,
    look_cotangent,
    hidden_state,
    context,
    motion_weight,
    row_gates,
    row_candidate,
    column_gates,
    column_candidate,
):
    tile_rows, tile_cols, channels = left_features.shape
    strip_rows, strip_cols = right_features.shape[:2]
    hidden_size = hidden_state.shape[-1]
    zs = lax.axis_size("z")
    cells = tile_rows * tile_cols
    pixels = 2 * zs * cells
    strip = strip_rows * strip_cols
    targets = lax.axis_size(SPREAD) * strip
    first_col = lax.axis_index(COL) * tile_cols

    place = jnp.stack(
        [
            lax.axis_index("yh") * (tile_rows * 2 * zs),
            first_col,
            lax.axis_index("core"),
            lax.axis_index(("z", "core")) * strip_cols,
            lax.axis_index("yh"),
        ]
    ).astype(I32)
    lefts, right = pack(cells, tile_cols, channels, zs)(
        left_features.reshape(cells, channels),
        look_cotangent.reshape(cells, -1),
        flow_offsets,
        right_features,
    )

    left_cot = lax.all_to_all(lefts, "z", 0, 0).reshape(pixels // 2, -1)
    right = jnp.concatenate([right, swap(right, "yh", 1)], axis=0)
    rights = jnp.broadcast_to(right[None], (lax.axis_size(COL),) + right.shape)
    left_cot, rights = lax.optimization_barrier((left_cot, rights))
    left_cot_other = swap(left_cot, "core", 1)
    right = lax.all_to_all(rights, COL, 0, 0).reshape(targets, channels)

    pool = jnp.asarray(pool_matrix(LANES, 2, strip_cols))
    spread, grad = spread_out(pixels, channels, targets, 64, targets // strip)(place, left_cot, left_cot_other, pool)
    outgoing, outgoing_other = look_up(pixels, channels, targets, 64)(
        place, left_cot, left_cot_other, right, spread, pool, motion_weight
    )

    outgoing = (outgoing + swap(outgoing_other, "core", 1).astype(F32)).astype(BF16)
    parts = lax.all_to_all(outgoing.reshape(zs, cells, 2 * channels), "z", 0, 0)
    parts, grad = lax.optimization_barrier((parts, grad))
    grad = lax.all_to_all(grad, SPREAD, 0, 0)
    grad_right = sum_parts(targets // strip, strip_rows, strip_cols, channels)(grad)

    joined, grad_left = add_up(zs, cells, channels, hidden_size)(
        parts, hidden_state.reshape(cells, hidden_size), context.reshape(cells, -1)
    )
    joined = joined.reshape(tile_rows, tile_cols, -1)
    joined = with_halo(with_halo(joined, ROW, 0, 4), COL, 1, 4)
    new_hidden = gru(tile_rows, tile_cols, hidden_size, row_gates.shape[0])(
        joined, row_gates, row_candidate, column_gates, column_candidate,
        warm(row_gates, row_candidate, column_gates, column_candidate),
    )
    return (
        new_hidden.reshape(hidden_state.shape),
        grad_left.reshape(left_features.shape),
        grad_right,
    )


def solution(mesh):
    mesh = jax.sharding.Mesh(mesh.devices.reshape(2, 8, 2, 4, 4), ROW + COL)
    tiled = P(ROW, COL, None)
    in_specs = (tiled, P(COL, ROW, None), P(None, ROW, None), tiled, tiled, tiled) + (P(),) * 5
    out_specs = (tiled, tiled, P(COL, ROW, None))
    return jax.shard_map(shards, mesh=mesh, in_specs=in_specs, out_specs=out_specs, check_vma=False)
```

```python
import jax
import jax.numpy as jnp
import numpy as np
from jax import lax
from jax.experimental import pallas as pl
from jax.experimental.pallas import tpu as pltpu
from jax.sharding import PartitionSpec as P

LEVELS = 4
RADIUS = 4
SIDE = 2 * RADIUS + 1
AREA = SIDE * SIDE
LANES = 128
F32 = jnp.float32
BF16 = jnp.bfloat16
I32 = jnp.int32


def iota(shape, dim):
    return lax.broadcasted_iota(I32, shape, dim)


def target_of(row, strip, col):
    return ((row >> 3) << 6) | (strip << 5) | ((row & 7) << 2) | col


def pool_matrix(rows, strips, width):
    count = np.arange(rows * strips * width)
    strip, row, col = count // (rows * width), count // width % rows, count % width
    target = target_of(row, strip, col)
    parts = []
    for level in (1, 2, 3):
        high, wide = rows >> level, max(width >> level, 1)
        cell = (strip * high + (row >> level)) * wide + (col >> level)
        part = np.zeros((strips * high * wide, count.size), np.float32)
        part[cell, target] = 0.25**level
        parts.append(part)
    pooled = np.concatenate(parts, axis=0)
    padded = -(-pooled.shape[0] // LANES) * LANES
    return np.pad(pooled, ((0, padded - pooled.shape[0]), (0, 0))).astype(BF16)


def take(values, index):
    return jnp.take_along_axis(values, index & (LANES - 1), axis=1, mode="promise_in_bounds")


def inside(index, count):
    return (index >= 0) & (index < count)


def pack(cells, tile_cols, channels, lefts):
    width = channels + LEVELS * AREA + 2

    def kernel(left_ref, cot_ref, flow_ref, right_ref, lefts_hbm, right_out, left, wide, sems):
        first_col = lax.axis_index(COL) * tile_cols
        for row in range(right_ref.shape[0]):
            step = right_ref.shape[1]
            wide[row * step : (row + 1) * step, :] = right_ref[row].astype(F32)
        right_out[...] = wide[...].astype(BF16)
        left[:, :channels] = left_ref[...]
        left[:, channels : width - 2] = cot_ref[...]
        chosen = iota((tile_cols, LANES), 1) == first_col + iota((tile_cols, LANES), 0)
        for axis in range(2):
            columns = []
            for row in range(cells // tile_cols):
                values = jnp.broadcast_to(flow_ref[axis, row : row + 1, :].astype(F32), (tile_cols, LANES))
                columns.append(jnp.sum(jnp.where(chosen, values, 0.0), axis=1, keepdims=True))
            column = jnp.concatenate(columns, axis=0).astype(BF16)
            left[:, width - 2 + axis : width - 1 + axis] = column
        copies = [pltpu.make_async_copy(left, lefts_hbm.at[i], sems.at[i]) for i in range(lefts)]
        for copy in copies:
            copy.start()
        for copy in copies:
            copy.wait()

    vmem, hbm = pl.BlockSpec(memory_space=pltpu.VMEM), pl.BlockSpec(memory_space=pltpu.HBM)
    return pl.pallas_call(
        kernel,
        out_shape=(
            jax.ShapeDtypeStruct((lefts, cells, width), BF16),
            jax.ShapeDtypeStruct((cells, channels), BF16),
        ),
        in_specs=[vmem] * 4,
        out_specs=[hbm, vmem],
        scratch_shapes=[
            pltpu.VMEM((cells, width), BF16),
            pltpu.VMEM((cells, channels), F32),
            pltpu.SemaphoreType.DMA((lefts,)),
        ],
        compiler_params=pltpu.CompilerParams(vmem_limit_bytes=60 * 2**20),
        name="pack",
    )


def centers_of(place, given, index, chunk):
    shape = (chunk, LANES)
    pixel = index * chunk + iota(shape, 0)
    core = place[2] ^ (pixel >> 8)
    row = place[0] + ((pixel >> 5) & 7) * 8 + core * 4 + ((pixel >> 3) & 3)
    col = place[1] + (pixel & 7)
    row = row + jnp.broadcast_to(given[:, LEVELS * AREA : LEVELS * AREA + 1], shape).astype(I32)
    col = col + jnp.broadcast_to(given[:, LEVELS * AREA + 1 : LEVELS * AREA + 2], shape).astype(I32)
    return [(row >> level, col >> level) for level in range(LEVELS)]


def spread_out(pixels, channels, targets, chunk, blocks):
    tiles = targets // LANES
    size = targets // blocks
    half = pixels // 2

    def kernel(
        place, own_ref, other_ref, pool_ref, spread_hbm, grad_hbm,
        left, rest, fine, coarse, spread_ref, grad_ref, sems,
    ):
        scale = channels**-0.5
        first = place[3]
        left[:half, :] = own_ref[:, :channels]
        left[half:, :] = other_ref[:, :channels]
        rest[:half, :] = own_ref[:, channels:]
        rest[half:, :] = other_ref[:, channels:]

        def step(index, carry):
            rows = pl.ds(pl.multiple_of(index * chunk, chunk), chunk)
            shape = (chunk, LANES)
            lane = iota(shape, 1)
            given = rest[rows, :].astype(F32)
            centers = centers_of(place, given, index, chunk)
            cots = []
            for level in range(LEVELS):
                part = given[:, level * AREA : (level + 1) * AREA]
                cots.append(jnp.pad(part, ((0, 0), (0, LANES - AREA))))

            def window(level, row, col):
                a, b = row - centers[level][0], col + (first >> level) - centers[level][1]
                valid = (jnp.abs(a) <= RADIUS) & (jnp.abs(b) <= RADIUS)
                return jnp.where(valid, take(cots[level], a * SIDE + b + AREA // 2), 0.0)

            flip = place[4]
            a = ((lane >> 6) << 3) + ((lane >> 2) & 7) - centers[0][0]
            b = ((((lane >> 5) & 1) ^ flip) << 6) + (lane & 3) + first - centers[0][1]
            near_col = jnp.abs(b) <= RADIUS
            entry = a * SIDE + b + AREA // 2
            for tile in range(tiles):
                valid = near_col & (jnp.abs(a + 16 * tile) <= RADIUS)
                picked = take(cots[0], entry + 16 * SIDE * tile)
                fine[rows, tile * LANES : (tile + 1) * LANES] = jnp.where(valid, picked, 0.0)
            for tile in range(2):
                cell = window(1, lane >> 1, ((tile ^ flip) << 5) + (lane & 1))
                coarse[rows, tile * LANES : (tile + 1) * LANES] = cell.astype(BF16)
            second = window(2, lane & 31, (((lane >> 5) & 1) ^ flip) << 4)
            third = window(3, lane & 15, (((lane >> 4) & 1) ^ flip) << 3)
            cell = jnp.where(lane < 64, second, jnp.where(lane < 96, third, 0.0))
            coarse[rows, 2 * LANES :] = cell.astype(BF16)
            return carry

        lax.fori_loop(0, pixels // chunk, step, 0)

        spread = (fine[...] + jnp.dot(coarse[...], pool_ref[...], preferred_element_type=F32)).astype(BF16)
        spread_ref[...] = spread
        spread_copy = pltpu.make_async_copy(spread_ref, spread_hbm, sems.at[0])
        spread_copy.start()
        grad_ref[...] = (
            lax.dot_general(spread, left[...], (((0,), (0,)), ((), ())), preferred_element_type=F32) * scale
        ).astype(BF16)
        grad_copies = []
        for block in range(blocks):
            owner = ((block & 1) ^ place[4]) * (blocks // 2) + (block >> 1)
            copy = pltpu.make_async_copy(
                grad_ref.at[block * size : (block + 1) * size], grad_hbm.at[owner], sems.at[1 + block]
            )
            copy.start()
            grad_copies.append(copy)
        spread_copy.wait()
        for copy in grad_copies:
            copy.wait()

    vmem, hbm = pl.BlockSpec(memory_space=pltpu.VMEM), pl.BlockSpec(memory_space=pltpu.HBM)
    return pl.pallas_call(
        kernel,
        out_shape=(
            jax.ShapeDtypeStruct((pixels, targets), BF16),
            jax.ShapeDtypeStruct((blocks, size, channels), BF16),
        ),
        in_specs=[pl.BlockSpec(memory_space=pltpu.SMEM)] + [vmem] * 3,
        out_specs=[hbm] * 2,
        scratch_shapes=[
            pltpu.VMEM((pixels, channels), BF16),
            pltpu.VMEM((pixels, LEVELS * AREA + 2), BF16),
            pltpu.VMEM((pixels, targets), F32),
            pltpu.VMEM((pixels, 3 * LANES), BF16),
            pltpu.VMEM((pixels, targets), BF16),
            pltpu.VMEM((targets, channels), BF16),
            pltpu.SemaphoreType.DMA((1 + blocks,)),
        ],
        compiler_params=pltpu.CompilerParams(vmem_limit_bytes=24 * 2**20),
        cost_estimate=pl.CostEstimate(flops=5 * 10**9, bytes_accessed=4 * 10**6, transcendentals=0),
        name="spread_out",
    )


def look_up(pixels, channels, targets, chunk):
    tiles = targets // LANES
    half = pixels // 2

    def kernel(
        place, own_ref, other_ref, right_ref, spread_hbm, pool_ref, motion_ref,
        out_own, out_other, left, rest, vol, looked, looked_low, weight, spread_ref, sem,
    ):
        spread_copy = pltpu.make_async_copy(spread_hbm, spread_ref, sem)
        spread_copy.start()
        scale = channels**-0.5
        first = place[3]
        left[:half, :] = own_ref[:, :channels]
        left[half:, :] = other_ref[:, :channels]
        rest[:half, :] = own_ref[:, channels:]
        rest[half:, :] = other_ref[:, channels:]
        weight[...] = jnp.zeros(weight.shape, F32)
        for level in range(LEVELS):
            weight[level * LANES : level * LANES + AREA, :] = motion_ref[level * AREA : (level + 1) * AREA, :]
        right = right_ref[...]
        contract_last = (((1,), (1,)), ((), ()))
        pooled = jnp.dot(pool_ref[...], right, preferred_element_type=F32)
        high = pooled.astype(BF16)
        low = (pooled - high.astype(F32)).astype(BF16)
        vol[:, :targets] = lax.dot_general(left[...], right, contract_last, preferred_element_type=F32)
        vol[:, targets:] = lax.dot_general(
            left[...], high, contract_last, preferred_element_type=F32
        ) + lax.dot_general(left[...], low, contract_last, preferred_element_type=F32)

        def step(index, carry):
            rows = pl.ds(pl.multiple_of(index * chunk, chunk), chunk)
            shape = (chunk, LANES)
            lane = iota(shape, 1)
            a_of = lane // SIDE
            b_of = lane - a_of * SIDE - RADIUS
            a_of = a_of - RADIUS
            in_window = lane < AREA
            centers = centers_of(place, rest[rows, :].astype(F32), index, chunk)
            for level in range(LEVELS):
                height, apart, width = LANES >> level, 64 >> level, max(4 >> level, 1)
                row = centers[level][0] + a_of
                col = centers[level][1] + b_of - (first >> level)
                within = col & (apart - 1)
                valid = inside(row, height) & inside(col, 2 * apart) & (within < width) & in_window
                strip = ((col >> (6 - level)) & 1) ^ place[4]
                start, count = ((0, tiles), (tiles, 2), (tiles + 2, 1), (tiles + 2, 1))[level]
                if level == 0:
                    cell = target_of(row, strip, within)
                else:
                    cell = (strip * height + row) * width + within + (64 if level == 3 else 0)
                which = jnp.where(valid, cell >> 7, -1)
                found = jnp.zeros(shape, F32)
                for tile in range(count):
                    at = (start + tile) * LANES
                    picked = take(vol[rows, at : at + LANES], cell)
                    found = jnp.where(which == tile, picked, found)
                found = found * scale
                upper = found.astype(BF16)
                looked[rows, level * LANES : (level + 1) * LANES] = upper
                looked_low[rows, level * LANES : (level + 1) * LANES] = (found - upper.astype(F32)).astype(BF16)
            return carry

        lax.fori_loop(0, pixels // chunk, step, 0)

        weight_high = weight[...].astype(BF16)
        weight_low = (weight[...] - weight_high.astype(F32)).astype(BF16)
        motion = jnp.dot(looked[...], weight_high, preferred_element_type=F32)
        motion = motion + jnp.dot(looked[...], weight_low, preferred_element_type=F32)
        motion = motion + jnp.dot(looked_low[...], weight_high, preferred_element_type=F32)
        spread_copy.wait()
        grad_left = jnp.dot(spread_ref[...], right, preferred_element_type=F32) * scale
        out_own[:, :channels] = motion[:half]
        out_own[:, channels:] = grad_left[:half]
        out_other[:, :channels] = motion[half:].astype(BF16)
        out_other[:, channels:] = grad_left[half:].astype(BF16)

    vmem, hbm = pl.BlockSpec(memory_space=pltpu.VMEM), pl.BlockSpec(memory_space=pltpu.HBM)
    return pl.pallas_call(
        kernel,
        out_shape=(
            jax.ShapeDtypeStruct((half, 2 * channels), F32),
            jax.ShapeDtypeStruct((half, 2 * channels), BF16),
        ),
        in_specs=[pl.BlockSpec(memory_space=pltpu.SMEM)] + [vmem] * 3 + [hbm] + [vmem] * 2,
        out_specs=[vmem] * 2,
        scratch_shapes=[
            pltpu.VMEM((pixels, channels), BF16),
            pltpu.VMEM((pixels, LEVELS * AREA + 2), BF16),
            pltpu.VMEM((pixels, targets + 3 * LANES), F32),
            pltpu.VMEM((pixels, LEVELS * LANES), BF16),
            pltpu.VMEM((pixels, LEVELS * LANES), BF16),
            pltpu.VMEM((LEVELS * LANES, channels), F32),
            pltpu.VMEM((pixels, targets), BF16),
            pltpu.SemaphoreType.DMA,
        ],
        compiler_params=pltpu.CompilerParams(vmem_limit_bytes=24 * 2**20),
        cost_estimate=pl.CostEstimate(flops=6 * 10**9, bytes_accessed=4 * 10**6, transcendentals=0),
        name="look_up",
    )


def add_up(parts, cells, channels, hidden_size):
    def kernel(parts_ref, hidden_ref, context_ref, joined_ref, grad_ref):
        total = parts_ref[0].astype(F32)
        for part in range(1, parts):
            total = total + parts_ref[part].astype(F32)
        joined_ref[:, :hidden_size] = hidden_ref[...]
        joined_ref[:, hidden_size : hidden_size + channels] = jnp.maximum(total[:, :channels], 0.0).astype(BF16)
        joined_ref[:, hidden_size + channels :] = context_ref[...]
        grad_ref[...] = total[:, channels:]

    vmem, hbm = pl.BlockSpec(memory_space=pltpu.VMEM), pl.BlockSpec(memory_space=pltpu.HBM)
    return pl.pallas_call(
        kernel,
        out_shape=(
            jax.ShapeDtypeStruct((cells, 2 * channels), BF16),
            jax.ShapeDtypeStruct((cells, channels), F32),
        ),
        in_specs=[vmem] * 3,
        out_specs=[vmem] * 2,
        compiler_params=pltpu.CompilerParams(vmem_limit_bytes=16 * 2**20),
        name="add_up",
    )


def sum_parts(parts, rows, cols, channels):
    def kernel(parts_ref, out_ref):
        total = parts_ref[0].astype(F32)
        for part in range(1, parts):
            total = total + parts_ref[part].astype(F32)
        for row in range(rows):
            out_ref[row] = total[row * cols : (row + 1) * cols]

    vmem = pl.BlockSpec(memory_space=pltpu.VMEM)
    return pl.pallas_call(
        kernel,
        out_shape=jax.ShapeDtypeStruct((rows, cols, channels), F32),
        in_specs=[vmem],
        out_specs=vmem,
        compiler_params=pltpu.CompilerParams(vmem_limit_bytes=16 * 2**20),
        name="sum_parts",
    )


def warm(*weights):
    def kernel(*refs):
        total = refs[0][0, :16, :LANES]
        for ref in refs[1:-1]:
            total = total + ref[0, :16, :LANES]
        refs[-1][...] = total

    vmem = pl.BlockSpec(memory_space=pltpu.VMEM)
    return pl.pallas_call(
        kernel,
        out_shape=jax.ShapeDtypeStruct((16, LANES), BF16),
        in_specs=[vmem] * len(weights),
        out_specs=vmem,
        compiler_params=pltpu.CompilerParams(vmem_limit_bytes=24 * 2**20),
        cost_estimate=pl.CostEstimate(flops=2 * 10**9, bytes_accessed=4 * 10**6, transcendentals=0),
        name="warm",
    )(*weights)


def gru(tile_rows, tile_cols, hidden_size, taps):
    high, wide = tile_rows + 8, tile_cols + 8

    def sigmoid(x):
        return 1.0 / (1.0 + jnp.exp(-x))

    def kernel(cells_ref, rg_ref, rc_ref, cg_ref, cc_ref, warm_ref, out_ref):
        flat = high * wide
        hidden_bf = cells_ref[:, :, :hidden_size].reshape(flat, hidden_size)
        inputs = cells_ref[:, :, hidden_size:].reshape(flat, -1)
        hidden = hidden_bf.astype(F32)

        def conv_x(source, weight_ref):
            total = None
            for tap in range(taps):
                product = jnp.dot(source, weight_ref[tap], preferred_element_type=F32)
                shift = (2 - tap) % flat
                if shift:
                    product = pltpu.roll(product, shift, 0)
                total = product if total is None else total + product
            return total

        gates = sigmoid(conv_x(jnp.concatenate([hidden_bf, inputs], axis=-1), rg_ref))
        update, reset = gates[:, :hidden_size], gates[:, hidden_size:]
        reset_state = (reset * hidden).astype(BF16)
        candidate = jnp.tanh(conv_x(jnp.concatenate([reset_state, inputs], axis=-1), rc_ref))
        middle = (1.0 - update) * hidden + update * candidate

        def own_columns(values):
            moved = pltpu.roll(values, flat - 4, 0).reshape(high, wide, -1)
            return moved[:, :tile_cols].reshape(high * tile_cols, -1)

        middle_bf = own_columns(middle).astype(BF16)
        inputs = own_columns(inputs.astype(F32)).astype(BF16)
        middle = middle_bf.astype(F32)

        def conv_y(source, weight_ref, count):
            total = None
            for tap in range(taps):
                product = jnp.dot(source, weight_ref[tap], preferred_element_type=F32)
                part = product[tap * tile_cols : (tap + count) * tile_cols]
                total = part if total is None else total + part
            return total

        gates = sigmoid(conv_y(jnp.concatenate([middle_bf, inputs], axis=-1), cg_ref, high - 4))
        reset = gates[:, hidden_size:]
        update = gates[2 * tile_cols : (2 + tile_rows) * tile_cols, :hidden_size]
        reset_state = (reset * middle[2 * tile_cols : (high - 2) * tile_cols]).astype(F32)
        edge = jnp.zeros((2 * tile_cols, hidden_size), F32)
        reset_state = jnp.concatenate([edge, reset_state, edge], axis=0).astype(BF16)
        joined = jnp.concatenate([reset_state, inputs], axis=-1)
        total = None
        for tap in range(taps):
            product = jnp.dot(joined, cc_ref[tap], preferred_element_type=F32)
            part = product[(tap + 2) * tile_cols : (tap + 2 + tile_rows) * tile_cols]
            total = part if total is None else total + part
        candidate = jnp.tanh(total)
        center = middle[4 * tile_cols : (4 + tile_rows) * tile_cols]
        out_ref[...] = (1.0 - update) * center + update * candidate

    return pl.pallas_call(
        kernel,
        out_shape=jax.ShapeDtypeStruct((tile_rows * tile_cols, hidden_size), F32),
        in_specs=[pl.BlockSpec(memory_space=pltpu.VMEM)] * 6,
        out_specs=pl.BlockSpec(memory_space=pltpu.VMEM),
        compiler_params=pltpu.CompilerParams(vmem_limit_bytes=24 * 2**20),
        cost_estimate=pl.CostEstimate(flops=10**9, bytes_accessed=5 * 10**6, transcendentals=10**5),
        name="gru",
    )


def with_halo(cells, axis, dim, width):
    count = lax.axis_size(axis)
    ends = count - 1
    head = lax.slice_in_dim(cells, 0, width, axis=dim)
    tail = lax.slice_in_dim(cells, cells.shape[dim] - width, cells.shape[dim], axis=dim)
    return jnp.concatenate(
        [
            lax.ppermute(tail, axis, [(i, (i + 1) % count) for i in range(ends)]),
            cells,
            lax.ppermute(head, axis, [((i + 1) % count, i) for i in range(ends)]),
        ],
        axis=dim,
    )


def swap(block, axis, bit):
    return lax.ppermute(block, axis, [(i, i ^ bit) for i in range(lax.axis_size(axis))])


ROW = ("yh", "z", "core")
COL = ("x", "yl")
SPREAD = ("yh", "x", "yl")


def shards(
    left_features,
    right_features,
    flow_offsets,
    look_cotangent,
    hidden_state,
    context,
    motion_weight,
    row_gates,
    row_candidate,
    column_gates,
    column_candidate,
):
    tile_rows, tile_cols, channels = left_features.shape
    strip_rows, strip_cols = right_features.shape[:2]
    hidden_size = hidden_state.shape[-1]
    zs = lax.axis_size("z")
    cells = tile_rows * tile_cols
    pixels = 2 * zs * cells
    strip = strip_rows * strip_cols
    targets = lax.axis_size(SPREAD) * strip
    first_col = lax.axis_index(COL) * tile_cols

    place = jnp.stack(
        [
            lax.axis_index("yh") * (tile_rows * 2 * zs),
            first_col,
            lax.axis_index("core"),
            lax.axis_index(("z", "core")) * strip_cols,
            lax.axis_index("yh"),
        ]
    ).astype(I32)
    lefts, right = pack(cells, tile_cols, channels, zs)(
        left_features.reshape(cells, channels),
        look_cotangent.reshape(cells, -1),
        flow_offsets,
        right_features,
    )

    left_cot = lax.all_to_all(lefts, "z", 0, 0).reshape(pixels // 2, -1)
    pair = (right, swap(right, "yh", 1))
    rights = jnp.concatenate(
        [jnp.broadcast_to(tile[None], (lax.axis_size(COL),) + tile.shape) for tile in pair], axis=1
    )
    left_cot, rights = lax.optimization_barrier((left_cot, rights))
    left_cot_other = swap(left_cot, "core", 1)
    right = lax.all_to_all(rights, COL, 0, 0).reshape(targets, channels)

    pool = jnp.asarray(pool_matrix(LANES, 2, strip_cols))
    spread, grad = spread_out(pixels, channels, targets, 64, targets // strip)(place, left_cot, left_cot_other, pool)
    outgoing, outgoing_other = look_up(pixels, channels, targets, 64)(
        place, left_cot, left_cot_other, right, spread, pool, motion_weight
    )

    outgoing = (outgoing + swap(outgoing_other, "core", 1).astype(F32)).astype(BF16)
    parts = lax.all_to_all(outgoing.reshape(zs, cells, 2 * channels), "z", 0, 0)
    joined, grad_left = add_up(zs, cells, channels, hidden_size)(
        parts, hidden_state.reshape(cells, hidden_size), context.reshape(cells, -1)
    )
    joined, grad = lax.optimization_barrier((joined, grad))
    grad = lax.all_to_all(grad, SPREAD, 0, 0)
    grad_right = sum_parts(targets // strip, strip_rows, strip_cols, channels)(grad)
    joined = joined.reshape(tile_rows, tile_cols, -1)
    joined = with_halo(with_halo(joined, ROW, 0, 4), COL, 1, 4)
    new_hidden = gru(tile_rows, tile_cols, hidden_size, row_gates.shape[0])(
        joined, row_gates, row_candidate, column_gates, column_candidate,
        warm(row_gates, row_candidate, column_gates, column_candidate),
    )
    return (
        new_hidden.reshape(hidden_state.shape),
        grad_left.reshape(left_features.shape),
        grad_right,
    )


def solution(mesh):
    mesh = jax.sharding.Mesh(mesh.devices.reshape(2, 8, 2, 4, 4), ROW + COL)
    tiled = P(ROW, COL, None)
    in_specs = (tiled, P(COL, ROW, None), P(None, ROW, None), tiled, tiled, tiled) + (P(),) * 5
    out_specs = (tiled, tiled, P(COL, ROW, None))
    return jax.shard_map(shards, mesh=mesh, in_specs=in_specs, out_specs=out_specs, check_vma=False)
```

```python
import jax
import jax.numpy as jnp
import numpy as np
from jax import lax
from jax.experimental import pallas as pl
from jax.experimental.pallas import tpu as pltpu
from jax.sharding import PartitionSpec as P

LEVELS = 4
RADIUS = 4
SIDE = 2 * RADIUS + 1
AREA = SIDE * SIDE
LANES = 128
F32 = jnp.float32
BF16 = jnp.bfloat16
I32 = jnp.int32


def iota(shape, dim):
    return lax.broadcasted_iota(I32, shape, dim)


def target_of(row, strip, col):
    return ((row >> 3) << 6) | (strip << 5) | ((row & 7) << 2) | col


def pool_matrix(rows, strips, width):
    count = np.arange(rows * strips * width)
    strip, row, col = count // (rows * width), count // width % rows, count % width
    target = target_of(row, strip, col)
    parts = []
    for level in (1, 2, 3):
        high, wide = rows >> level, max(width >> level, 1)
        cell = (strip * high + (row >> level)) * wide + (col >> level)
        part = np.zeros((strips * high * wide, count.size), np.float32)
        part[cell, target] = 0.25**level
        parts.append(part)
    pooled = np.concatenate(parts, axis=0)
    padded = -(-pooled.shape[0] // LANES) * LANES
    return np.pad(pooled, ((0, padded - pooled.shape[0]), (0, 0))).astype(BF16)


def take(values, index):
    return jnp.take_along_axis(values, index & (LANES - 1), axis=1, mode="promise_in_bounds")


def inside(index, count):
    return (index >= 0) & (index < count)


def pack(cells, tile_cols, channels, lefts):
    width = channels + LEVELS * AREA + 2

    def kernel(left_ref, cot_ref, flow_ref, right_ref, lefts_hbm, right_out, left, wide, sems):
        first_col = lax.axis_index(COL) * tile_cols
        for row in range(right_ref.shape[0]):
            step = right_ref.shape[1]
            wide[row * step : (row + 1) * step, :] = right_ref[row].astype(F32)
        right_out[...] = wide[...].astype(BF16)
        left[:, :channels] = left_ref[...]
        left[:, channels : width - 2] = cot_ref[...]
        chosen = iota((tile_cols, LANES), 1) == first_col + iota((tile_cols, LANES), 0)
        for axis in range(2):
            columns = []
            for row in range(cells // tile_cols):
                values = jnp.broadcast_to(flow_ref[axis, row : row + 1, :].astype(F32), (tile_cols, LANES))
                columns.append(jnp.sum(jnp.where(chosen, values, 0.0), axis=1, keepdims=True))
            column = jnp.concatenate(columns, axis=0).astype(BF16)
            left[:, width - 2 + axis : width - 1 + axis] = column
        copies = [pltpu.make_async_copy(left, lefts_hbm.at[i], sems.at[i]) for i in range(lefts)]
        for copy in copies:
            copy.start()
        for copy in copies:
            copy.wait()

    vmem, hbm = pl.BlockSpec(memory_space=pltpu.VMEM), pl.BlockSpec(memory_space=pltpu.HBM)
    return pl.pallas_call(
        kernel,
        out_shape=(
            jax.ShapeDtypeStruct((lefts, cells, width), BF16),
            jax.ShapeDtypeStruct((cells, channels), BF16),
        ),
        in_specs=[vmem] * 4,
        out_specs=[hbm, vmem],
        scratch_shapes=[
            pltpu.VMEM((cells, width), BF16),
            pltpu.VMEM((cells, channels), F32),
            pltpu.SemaphoreType.DMA((lefts,)),
        ],
        compiler_params=pltpu.CompilerParams(vmem_limit_bytes=60 * 2**20),
        name="pack",
    )


def centers_of(place, given, index, chunk):
    shape = (chunk, LANES)
    pixel = index * chunk + iota(shape, 0)
    core = place[2] ^ (pixel >> 8)
    row = place[0] + ((pixel >> 5) & 7) * 8 + core * 4 + ((pixel >> 3) & 3)
    col = place[1] + (pixel & 7)
    row = row + jnp.broadcast_to(given[:, LEVELS * AREA : LEVELS * AREA + 1], shape).astype(I32)
    col = col + jnp.broadcast_to(given[:, LEVELS * AREA + 1 : LEVELS * AREA + 2], shape).astype(I32)
    return [(row >> level, col >> level) for level in range(LEVELS)]


def spread_out(pixels, channels, targets, chunk, blocks):
    tiles = targets // LANES
    size = targets // blocks
    half = pixels // 2

    def kernel(
        place, own_ref, other_ref, pool_ref, spread_hbm, grad_hbm,
        left, rest, fine, coarse, spread_ref, grad_ref, sems,
    ):
        scale = channels**-0.5
        first = place[3]
        left[:half, :] = own_ref[:, :channels]
        left[half:, :] = other_ref[:, :channels]
        rest[:half, :] = own_ref[:, channels:]
        rest[half:, :] = other_ref[:, channels:]

        def step(index, carry):
            rows = pl.ds(pl.multiple_of(index * chunk, chunk), chunk)
            shape = (chunk, LANES)
            lane = iota(shape, 1)
            given = rest[rows, :].astype(F32)
            centers = centers_of(place, given, index, chunk)
            cots = []
            for level in range(LEVELS):
                part = given[:, level * AREA : (level + 1) * AREA]
                cots.append(jnp.pad(part, ((0, 0), (0, LANES - AREA))))

            def window(level, row, col):
                a, b = row - centers[level][0], col + (first >> level) - centers[level][1]
                valid = (jnp.abs(a) <= RADIUS) & (jnp.abs(b) <= RADIUS)
                return jnp.where(valid, take(cots[level], a * SIDE + b + AREA // 2), 0.0)

            flip = place[4]
            a = ((lane >> 6) << 3) + ((lane >> 2) & 7) - centers[0][0]
            b = ((((lane >> 5) & 1) ^ flip) << 6) + (lane & 3) + first - centers[0][1]
            near_col = jnp.abs(b) <= RADIUS
            entry = a * SIDE + b + AREA // 2
            for tile in range(tiles):
                valid = near_col & (jnp.abs(a + 16 * tile) <= RADIUS)
                picked = take(cots[0], entry + 16 * SIDE * tile)
                fine[rows, tile * LANES : (tile + 1) * LANES] = jnp.where(valid, picked, 0.0)
            for tile in range(2):
                cell = window(1, lane >> 1, ((tile ^ flip) << 5) + (lane & 1))
                coarse[rows, tile * LANES : (tile + 1) * LANES] = cell.astype(BF16)
            second = window(2, lane & 31, (((lane >> 5) & 1) ^ flip) << 4)
            third = window(3, lane & 15, (((lane >> 4) & 1) ^ flip) << 3)
            cell = jnp.where(lane < 64, second, jnp.where(lane < 96, third, 0.0))
            coarse[rows, 2 * LANES :] = cell.astype(BF16)
            return carry

        lax.fori_loop(0, pixels // chunk, step, 0)

        spread = (fine[...] + jnp.dot(coarse[...], pool_ref[...], preferred_element_type=F32)).astype(BF16)
        spread_ref[...] = spread
        spread_copy = pltpu.make_async_copy(spread_ref, spread_hbm, sems.at[0])
        spread_copy.start()
        grad_ref[...] = (
            lax.dot_general(spread, left[...], (((0,), (0,)), ((), ())), preferred_element_type=F32) * scale
        ).astype(BF16)
        grad_copies = []
        for block in range(blocks):
            owner = ((block & 1) ^ place[4]) * (blocks // 2) + (block >> 1)
            copy = pltpu.make_async_copy(
                grad_ref.at[block * size : (block + 1) * size], grad_hbm.at[owner], sems.at[1 + block]
            )
            copy.start()
            grad_copies.append(copy)
        spread_copy.wait()
        for copy in grad_copies:
            copy.wait()

    vmem, hbm = pl.BlockSpec(memory_space=pltpu.VMEM), pl.BlockSpec(memory_space=pltpu.HBM)
    return pl.pallas_call(
        kernel,
        out_shape=(
            jax.ShapeDtypeStruct((pixels, targets), BF16),
            jax.ShapeDtypeStruct((blocks, size, channels), BF16),
        ),
        in_specs=[pl.BlockSpec(memory_space=pltpu.SMEM)] + [vmem] * 3,
        out_specs=[hbm] * 2,
        scratch_shapes=[
            pltpu.VMEM((pixels, channels), BF16),
            pltpu.VMEM((pixels, LEVELS * AREA + 2), BF16),
            pltpu.VMEM((pixels, targets), F32),
            pltpu.VMEM((pixels, 3 * LANES), BF16),
            pltpu.VMEM((pixels, targets), BF16),
            pltpu.VMEM((targets, channels), BF16),
            pltpu.SemaphoreType.DMA((1 + blocks,)),
        ],
        compiler_params=pltpu.CompilerParams(vmem_limit_bytes=24 * 2**20),
        cost_estimate=pl.CostEstimate(flops=5 * 10**9, bytes_accessed=4 * 10**6, transcendentals=0),
        name="spread_out",
    )


def look_up(pixels, channels, targets, chunk):
    tiles = targets // LANES
    half = pixels // 2

    def kernel(
        place, own_ref, other_ref, right_ref, spread_hbm, pool_ref, motion_ref,
        out_own, out_other, left, rest, vol, looked, looked_low, weight, spread_ref, sem,
    ):
        spread_copy = pltpu.make_async_copy(spread_hbm, spread_ref, sem)
        spread_copy.start()
        scale = channels**-0.5
        first = place[3]
        left[:half, :] = own_ref[:, :channels]
        left[half:, :] = other_ref[:, :channels]
        rest[:half, :] = own_ref[:, channels:]
        rest[half:, :] = other_ref[:, channels:]
        weight[...] = jnp.zeros(weight.shape, F32)
        for level in range(LEVELS):
            weight[level * LANES : level * LANES + AREA, :] = motion_ref[level * AREA : (level + 1) * AREA, :]
        right = right_ref[...]
        contract_last = (((1,), (1,)), ((), ()))
        pooled = jnp.dot(pool_ref[...], right, preferred_element_type=F32)
        high = pooled.astype(BF16)
        low = (pooled - high.astype(F32)).astype(BF16)
        vol[:, :targets] = lax.dot_general(left[...], right, contract_last, preferred_element_type=F32)
        vol[:, targets:] = lax.dot_general(
            left[...], high, contract_last, preferred_element_type=F32
        ) + lax.dot_general(left[...], low, contract_last, preferred_element_type=F32)

        def step(index, carry):
            rows = pl.ds(pl.multiple_of(index * chunk, chunk), chunk)
            shape = (chunk, LANES)
            lane = iota(shape, 1)
            a_of = lane // SIDE
            b_of = lane - a_of * SIDE - RADIUS
            a_of = a_of - RADIUS
            in_window = lane < AREA
            centers = centers_of(place, rest[rows, :].astype(F32), index, chunk)
            for level in range(LEVELS):
                height, apart, width = LANES >> level, 64 >> level, max(4 >> level, 1)
                row = centers[level][0] + a_of
                col = centers[level][1] + b_of - (first >> level)
                within = col & (apart - 1)
                valid = inside(row, height) & inside(col, 2 * apart) & (within < width) & in_window
                strip = ((col >> (6 - level)) & 1) ^ place[4]
                start, count = ((0, tiles), (tiles, 2), (tiles + 2, 1), (tiles + 2, 1))[level]
                if level == 0:
                    cell = target_of(row, strip, within)
                else:
                    cell = (strip * height + row) * width + within + (64 if level == 3 else 0)
                which = jnp.where(valid, cell >> 7, -1)
                found = jnp.zeros(shape, F32)
                for tile in range(count):
                    at = (start + tile) * LANES
                    picked = take(vol[rows, at : at + LANES], cell)
                    found = jnp.where(which == tile, picked, found)
                found = found * scale
                upper = found.astype(BF16)
                looked[rows, level * LANES : (level + 1) * LANES] = upper
                looked_low[rows, level * LANES : (level + 1) * LANES] = (found - upper.astype(F32)).astype(BF16)
            return carry

        lax.fori_loop(0, pixels // chunk, step, 0)

        weight_high = weight[...].astype(BF16)
        weight_low = (weight[...] - weight_high.astype(F32)).astype(BF16)
        motion = jnp.dot(looked[...], weight_high, preferred_element_type=F32)
        motion = motion + jnp.dot(looked[...], weight_low, preferred_element_type=F32)
        motion = motion + jnp.dot(looked_low[...], weight_high, preferred_element_type=F32)
        spread_copy.wait()
        grad_left = jnp.dot(spread_ref[...], right, preferred_element_type=F32) * scale
        out_own[:, :channels] = motion[:half]
        out_own[:, channels:] = grad_left[:half]
        out_other[:, :channels] = motion[half:].astype(BF16)
        out_other[:, channels:] = grad_left[half:].astype(BF16)

    vmem, hbm = pl.BlockSpec(memory_space=pltpu.VMEM), pl.BlockSpec(memory_space=pltpu.HBM)
    return pl.pallas_call(
        kernel,
        out_shape=(
            jax.ShapeDtypeStruct((half, 2 * channels), F32),
            jax.ShapeDtypeStruct((half, 2 * channels), BF16),
        ),
        in_specs=[pl.BlockSpec(memory_space=pltpu.SMEM)] + [vmem] * 3 + [hbm] + [vmem] * 2,
        out_specs=[vmem] * 2,
        scratch_shapes=[
            pltpu.VMEM((pixels, channels), BF16),
            pltpu.VMEM((pixels, LEVELS * AREA + 2), BF16),
            pltpu.VMEM((pixels, targets + 3 * LANES), F32),
            pltpu.VMEM((pixels, LEVELS * LANES), BF16),
            pltpu.VMEM((pixels, LEVELS * LANES), BF16),
            pltpu.VMEM((LEVELS * LANES, channels), F32),
            pltpu.VMEM((pixels, targets), BF16),
            pltpu.SemaphoreType.DMA,
        ],
        compiler_params=pltpu.CompilerParams(vmem_limit_bytes=24 * 2**20),
        cost_estimate=pl.CostEstimate(flops=6 * 10**9, bytes_accessed=4 * 10**6, transcendentals=0),
        name="look_up",
    )


def add_up(parts, cells, channels, hidden_size):
    def kernel(parts_ref, hidden_ref, context_ref, joined_ref, grad_ref):
        total = parts_ref[0].astype(F32)
        for part in range(1, parts):
            total = total + parts_ref[part].astype(F32)
        joined_ref[:, :hidden_size] = hidden_ref[...]
        joined_ref[:, hidden_size : hidden_size + channels] = jnp.maximum(total[:, :channels], 0.0).astype(BF16)
        joined_ref[:, hidden_size + channels :] = context_ref[...]
        grad_ref[...] = total[:, channels:]

    vmem, hbm = pl.BlockSpec(memory_space=pltpu.VMEM), pl.BlockSpec(memory_space=pltpu.HBM)
    return pl.pallas_call(
        kernel,
        out_shape=(
            jax.ShapeDtypeStruct((cells, 2 * channels), BF16),
            jax.ShapeDtypeStruct((cells, channels), F32),
        ),
        in_specs=[vmem] * 3,
        out_specs=[vmem] * 2,
        compiler_params=pltpu.CompilerParams(vmem_limit_bytes=16 * 2**20),
        name="add_up",
    )


def sum_parts(parts, rows, cols, channels):
    def kernel(parts_ref, out_ref):
        total = parts_ref[0].astype(F32)
        for part in range(1, parts):
            total = total + parts_ref[part].astype(F32)
        for row in range(rows):
            out_ref[row] = total[row * cols : (row + 1) * cols]

    vmem = pl.BlockSpec(memory_space=pltpu.VMEM)
    return pl.pallas_call(
        kernel,
        out_shape=jax.ShapeDtypeStruct((rows, cols, channels), F32),
        in_specs=[vmem],
        out_specs=vmem,
        compiler_params=pltpu.CompilerParams(vmem_limit_bytes=16 * 2**20),
        name="sum_parts",
    )


def warm(*weights):
    def kernel(*refs):
        total = refs[0][0, :16, :LANES]
        for ref in refs[1:-1]:
            total = total + ref[0, :16, :LANES]
        refs[-1][...] = total

    vmem = pl.BlockSpec(memory_space=pltpu.VMEM)
    return pl.pallas_call(
        kernel,
        out_shape=jax.ShapeDtypeStruct((16, LANES), BF16),
        in_specs=[vmem] * len(weights),
        out_specs=vmem,
        compiler_params=pltpu.CompilerParams(vmem_limit_bytes=24 * 2**20),
        cost_estimate=pl.CostEstimate(flops=2 * 10**9, bytes_accessed=4 * 10**6, transcendentals=0),
        name="warm",
    )(*weights)


def gru(tile_rows, tile_cols, hidden_size, taps):
    high, wide = tile_rows + 8, tile_cols + 8

    def sigmoid(x):
        return 1.0 / (1.0 + jnp.exp(-x))

    def kernel(cells_ref, rg_ref, rc_ref, cg_ref, cc_ref, warm_ref, out_ref):
        flat = high * wide
        hidden_bf = cells_ref[:, :, :hidden_size].reshape(flat, hidden_size)
        inputs = cells_ref[:, :, hidden_size:].reshape(flat, -1)
        hidden = hidden_bf.astype(F32)

        def conv_x(source, weight_ref):
            total = None
            for tap in range(taps):
                product = jnp.dot(source, weight_ref[tap], preferred_element_type=F32)
                shift = (2 - tap) % flat
                if shift:
                    product = pltpu.roll(product, shift, 0)
                total = product if total is None else total + product
            return total

        gates = sigmoid(conv_x(jnp.concatenate([hidden_bf, inputs], axis=-1), rg_ref))
        update, reset = gates[:, :hidden_size], gates[:, hidden_size:]
        reset_state = (reset * hidden).astype(BF16)
        candidate = jnp.tanh(conv_x(jnp.concatenate([reset_state, inputs], axis=-1), rc_ref))
        middle = (1.0 - update) * hidden + update * candidate

        def own_columns(values):
            moved = pltpu.roll(values, flat - 4, 0).reshape(high, wide, -1)
            return moved[:, :tile_cols].reshape(high * tile_cols, -1)

        middle_bf = own_columns(middle).astype(BF16)
        inputs = own_columns(inputs.astype(F32)).astype(BF16)
        middle = middle_bf.astype(F32)

        def conv_y(source, weight_ref, count):
            total = None
            for tap in range(taps):
                product = jnp.dot(source, weight_ref[tap], preferred_element_type=F32)
                part = product[tap * tile_cols : (tap + count) * tile_cols]
                total = part if total is None else total + part
            return total

        gates = sigmoid(conv_y(jnp.concatenate([middle_bf, inputs], axis=-1), cg_ref, high - 4))
        reset = gates[:, hidden_size:]
        update = gates[2 * tile_cols : (2 + tile_rows) * tile_cols, :hidden_size]
        reset_state = (reset * middle[2 * tile_cols : (high - 2) * tile_cols]).astype(F32)
        edge = jnp.zeros((2 * tile_cols, hidden_size), F32)
        reset_state = jnp.concatenate([edge, reset_state, edge], axis=0).astype(BF16)
        joined = jnp.concatenate([reset_state, inputs], axis=-1)
        total = None
        for tap in range(taps):
            product = jnp.dot(joined, cc_ref[tap], preferred_element_type=F32)
            part = product[(tap + 2) * tile_cols : (tap + 2 + tile_rows) * tile_cols]
            total = part if total is None else total + part
        candidate = jnp.tanh(total)
        center = middle[4 * tile_cols : (4 + tile_rows) * tile_cols]
        out_ref[...] = (1.0 - update) * center + update * candidate

    return pl.pallas_call(
        kernel,
        out_shape=jax.ShapeDtypeStruct((tile_rows * tile_cols, hidden_size), F32),
        in_specs=[pl.BlockSpec(memory_space=pltpu.VMEM)] * 6,
        out_specs=pl.BlockSpec(memory_space=pltpu.VMEM),
        compiler_params=pltpu.CompilerParams(vmem_limit_bytes=24 * 2**20),
        cost_estimate=pl.CostEstimate(flops=10**9, bytes_accessed=5 * 10**6, transcendentals=10**5),
        name="gru",
    )


def with_halo(cells, axis, dim, width):
    count = lax.axis_size(axis)
    ends = count - 1
    head = lax.slice_in_dim(cells, 0, width, axis=dim)
    tail = lax.slice_in_dim(cells, cells.shape[dim] - width, cells.shape[dim], axis=dim)
    return jnp.concatenate(
        [
            lax.ppermute(tail, axis, [(i, (i + 1) % count) for i in range(ends)]),
            cells,
            lax.ppermute(head, axis, [((i + 1) % count, i) for i in range(ends)]),
        ],
        axis=dim,
    )


def swap(block, axis, bit):
    return lax.ppermute(block, axis, [(i, i ^ bit) for i in range(lax.axis_size(axis))])


ROW = ("yh", "z", "core")
COL = ("x", "yl")
SPREAD = ("yh", "x", "yl")


def shards(
    left_features,
    right_features,
    flow_offsets,
    look_cotangent,
    hidden_state,
    context,
    motion_weight,
    row_gates,
    row_candidate,
    column_gates,
    column_candidate,
):
    tile_rows, tile_cols, channels = left_features.shape
    strip_rows, strip_cols = right_features.shape[:2]
    hidden_size = hidden_state.shape[-1]
    zs = lax.axis_size("z")
    cells = tile_rows * tile_cols
    pixels = 2 * zs * cells
    strip = strip_rows * strip_cols
    targets = lax.axis_size(SPREAD) * strip
    first_col = lax.axis_index(COL) * tile_cols

    place = jnp.stack(
        [
            lax.axis_index("yh") * (tile_rows * 2 * zs),
            first_col,
            lax.axis_index("core"),
            lax.axis_index(("z", "core")) * strip_cols,
            lax.axis_index("yh"),
        ]
    ).astype(I32)
    lefts, right = pack(cells, tile_cols, channels, zs)(
        left_features.reshape(cells, channels),
        look_cotangent.reshape(cells, -1),
        flow_offsets,
        right_features,
    )

    left_cot = lax.all_to_all(lefts, "z", 0, 0).reshape(pixels // 2, -1)
    pair = (right, swap(right, "yh", 1))
    rights = jnp.concatenate(
        [jnp.broadcast_to(tile[None], (lax.axis_size(COL),) + tile.shape) for tile in pair], axis=1
    )
    left_cot, rights = lax.optimization_barrier((left_cot, rights))
    left_cot_other = swap(left_cot, "core", 1)
    right = lax.all_to_all(rights, COL, 0, 0).reshape(targets, channels)

    pool = jnp.asarray(pool_matrix(LANES, 2, strip_cols))
    spread, grad = spread_out(pixels, channels, targets, 32, targets // strip)(place, left_cot, left_cot_other, pool)
    outgoing, outgoing_other = look_up(pixels, channels, targets, 32)(
        place, left_cot, left_cot_other, right, spread, pool, motion_weight
    )

    outgoing = (outgoing + swap(outgoing_other, "core", 1).astype(F32)).astype(BF16)
    parts = lax.all_to_all(outgoing.reshape(zs, cells, 2 * channels), "z", 0, 0)
    parts, grad = lax.optimization_barrier((parts, grad))
    grad = lax.all_to_all(grad, SPREAD, 0, 0)
    grad_right = sum_parts(targets // strip, strip_rows, strip_cols, channels)(grad)

    joined, grad_left = add_up(zs, cells, channels, hidden_size)(
        parts, hidden_state.reshape(cells, hidden_size), context.reshape(cells, -1)
    )
    joined = joined.reshape(tile_rows, tile_cols, -1)
    joined = with_halo(with_halo(joined, ROW, 0, 4), COL, 1, 4)
    new_hidden = gru(tile_rows, tile_cols, hidden_size, row_gates.shape[0])(
        joined, row_gates, row_candidate, column_gates, column_candidate,
        warm(row_gates, row_candidate, column_gates, column_candidate),
    )
    return (
        new_hidden.reshape(hidden_state.shape),
        grad_left.reshape(left_features.shape),
        grad_right,
    )


def solution(mesh):
    mesh = jax.sharding.Mesh(mesh.devices.reshape(2, 8, 2, 4, 4), ROW + COL)
    tiled = P(ROW, COL, None)
    in_specs = (tiled, P(COL, ROW, None), P(None, ROW, None), tiled, tiled, tiled) + (P(),) * 5
    out_specs = (tiled, tiled, P(COL, ROW, None))
    return jax.shard_map(shards, mesh=mesh, in_specs=in_specs, out_specs=out_specs, check_vma=False)
```

```python
import jax
import jax.numpy as jnp
import numpy as np
from jax import lax
from jax.experimental import pallas as pl
from jax.experimental.pallas import tpu as pltpu
from jax.sharding import PartitionSpec as P

LEVELS = 4
RADIUS = 4
SIDE = 2 * RADIUS + 1
AREA = SIDE * SIDE
LANES = 128
F32 = jnp.float32
BF16 = jnp.bfloat16
I32 = jnp.int32


def iota(shape, dim):
    return lax.broadcasted_iota(I32, shape, dim)


def target_of(row, strip, col):
    return ((row >> 3) << 6) | (strip << 5) | ((row & 7) << 2) | col


def pool_matrix(rows, strips, width):
    count = np.arange(rows * strips * width)
    strip, row, col = count // (rows * width), count // width % rows, count % width
    target = target_of(row, strip, col)
    parts = []
    for level in (1, 2, 3):
        high, wide = rows >> level, max(width >> level, 1)
        cell = (strip * high + (row >> level)) * wide + (col >> level)
        part = np.zeros((strips * high * wide, count.size), np.float32)
        part[cell, target] = 0.25**level
        parts.append(part)
    pooled = np.concatenate(parts, axis=0)
    padded = -(-pooled.shape[0] // LANES) * LANES
    return np.pad(pooled, ((0, padded - pooled.shape[0]), (0, 0))).astype(BF16)


def take(values, index):
    return jnp.take_along_axis(values, index & (LANES - 1), axis=1, mode="promise_in_bounds")


def inside(index, count):
    return (index >= 0) & (index < count)


def pack(cells, tile_cols, channels, lefts):
    width = channels + LEVELS * AREA + 2

    def kernel(left_ref, cot_ref, flow_ref, right_ref, lefts_hbm, right_out, left, wide, sems):
        first_col = lax.axis_index(COL) * tile_cols
        for row in range(right_ref.shape[0]):
            step = right_ref.shape[1]
            wide[row * step : (row + 1) * step, :] = right_ref[row].astype(F32)
        right_out[...] = wide[...].astype(BF16)
        left[:, :channels] = left_ref[...]
        left[:, channels : width - 2] = cot_ref[...]
        chosen = iota((tile_cols, LANES), 1) == first_col + iota((tile_cols, LANES), 0)
        for axis in range(2):
            columns = []
            for row in range(cells // tile_cols):
                values = jnp.broadcast_to(flow_ref[axis, row : row + 1, :].astype(F32), (tile_cols, LANES))
                columns.append(jnp.sum(jnp.where(chosen, values, 0.0), axis=1, keepdims=True))
            column = jnp.concatenate(columns, axis=0).astype(BF16)
            left[:, width - 2 + axis : width - 1 + axis] = column
        copies = [pltpu.make_async_copy(left, lefts_hbm.at[i], sems.at[i]) for i in range(lefts)]
        for copy in copies:
            copy.start()
        for copy in copies:
            copy.wait()

    vmem, hbm = pl.BlockSpec(memory_space=pltpu.VMEM), pl.BlockSpec(memory_space=pltpu.HBM)
    return pl.pallas_call(
        kernel,
        out_shape=(
            jax.ShapeDtypeStruct((lefts, cells, width), BF16),
            jax.ShapeDtypeStruct((cells, channels), BF16),
        ),
        in_specs=[vmem] * 4,
        out_specs=[hbm, vmem],
        scratch_shapes=[
            pltpu.VMEM((cells, width), BF16),
            pltpu.VMEM((cells, channels), F32),
            pltpu.SemaphoreType.DMA((lefts,)),
        ],
        compiler_params=pltpu.CompilerParams(vmem_limit_bytes=60 * 2**20),
        name="pack",
    )


def centers_of(place, given, index, chunk):
    shape = (chunk, LANES)
    pixel = index * chunk + iota(shape, 0)
    core = place[2] ^ (pixel >> 8)
    row = place[0] + ((pixel >> 5) & 7) * 8 + core * 4 + ((pixel >> 3) & 3)
    col = place[1] + (pixel & 7)
    row = row + jnp.broadcast_to(given[:, LEVELS * AREA : LEVELS * AREA + 1], shape).astype(I32)
    col = col + jnp.broadcast_to(given[:, LEVELS * AREA + 1 : LEVELS * AREA + 2], shape).astype(I32)
    return [(row >> level, col >> level) for level in range(LEVELS)]


def spread_out(pixels, channels, targets, chunk, blocks):
    tiles = targets // LANES
    size = targets // blocks
    half = pixels // 2

    def kernel(
        place, own_ref, other_ref, pool_ref, spread_hbm, grad_hbm,
        left, rest, fine, coarse, spread_ref, grad_ref, sems,
    ):
        scale = channels**-0.5
        first = place[3]
        left[:half, :] = own_ref[:, :channels]
        left[half:, :] = other_ref[:, :channels]
        rest[:half, :] = own_ref[:, channels:]
        rest[half:, :] = other_ref[:, channels:]

        def step(index, carry):
            rows = pl.ds(pl.multiple_of(index * chunk, chunk), chunk)
            shape = (chunk, LANES)
            lane = iota(shape, 1)
            given = rest[rows, :].astype(F32)
            centers = centers_of(place, given, index, chunk)
            cots = []
            for level in range(LEVELS):
                part = given[:, level * AREA : (level + 1) * AREA]
                cots.append(jnp.pad(part, ((0, 0), (0, LANES - AREA))))

            def window(level, row, col):
                a, b = row - centers[level][0], col + (first >> level) - centers[level][1]
                valid = (jnp.abs(a) <= RADIUS) & (jnp.abs(b) <= RADIUS)
                return jnp.where(valid, take(cots[level], a * SIDE + b + AREA // 2), 0.0)

            flip = place[4]
            a = ((lane >> 6) << 3) + ((lane >> 2) & 7) - centers[0][0]
            b = ((((lane >> 5) & 1) ^ flip) << 6) + (lane & 3) + first - centers[0][1]
            near_col = jnp.abs(b) <= RADIUS
            entry = a * SIDE + b + AREA // 2
            for tile in range(tiles):
                valid = near_col & (jnp.abs(a + 16 * tile) <= RADIUS)
                picked = take(cots[0], entry + 16 * SIDE * tile)
                fine[rows, tile * LANES : (tile + 1) * LANES] = jnp.where(valid, picked, 0.0)
            for tile in range(2):
                cell = window(1, lane >> 1, ((tile ^ flip) << 5) + (lane & 1))
                coarse[rows, tile * LANES : (tile + 1) * LANES] = cell.astype(BF16)
            second = window(2, lane & 31, (((lane >> 5) & 1) ^ flip) << 4)
            third = window(3, lane & 15, (((lane >> 4) & 1) ^ flip) << 3)
            cell = jnp.where(lane < 64, second, jnp.where(lane < 96, third, 0.0))
            coarse[rows, 2 * LANES :] = cell.astype(BF16)
            return carry

        lax.fori_loop(0, pixels // chunk, step, 0)

        spread = (fine[...] + jnp.dot(coarse[...], pool_ref[...], preferred_element_type=F32)).astype(BF16)
        spread_ref[...] = spread
        spread_copy = pltpu.make_async_copy(spread_ref, spread_hbm, sems.at[0])
        spread_copy.start()
        grad_ref[...] = (
            lax.dot_general(spread, left[...], (((0,), (0,)), ((), ())), preferred_element_type=F32) * scale
        ).astype(BF16)
        grad_copies = []
        for block in range(blocks):
            owner = ((block & 1) ^ place[4]) * (blocks // 2) + (block >> 1)
            copy = pltpu.make_async_copy(
                grad_ref.at[block * size : (block + 1) * size], grad_hbm.at[owner], sems.at[1 + block]
            )
            copy.start()
            grad_copies.append(copy)
        spread_copy.wait()
        for copy in grad_copies:
            copy.wait()

    vmem, hbm = pl.BlockSpec(memory_space=pltpu.VMEM), pl.BlockSpec(memory_space=pltpu.HBM)
    return pl.pallas_call(
        kernel,
        out_shape=(
            jax.ShapeDtypeStruct((pixels, targets), BF16),
            jax.ShapeDtypeStruct((blocks, size, channels), BF16),
        ),
        in_specs=[pl.BlockSpec(memory_space=pltpu.SMEM)] + [vmem] * 3,
        out_specs=[hbm] * 2,
        scratch_shapes=[
            pltpu.VMEM((pixels, channels), BF16),
            pltpu.VMEM((pixels, LEVELS * AREA + 2), BF16),
            pltpu.VMEM((pixels, targets), F32),
            pltpu.VMEM((pixels, 3 * LANES), BF16),
            pltpu.VMEM((pixels, targets), BF16),
            pltpu.VMEM((targets, channels), BF16),
            pltpu.SemaphoreType.DMA((1 + blocks,)),
        ],
        compiler_params=pltpu.CompilerParams(vmem_limit_bytes=24 * 2**20),
        cost_estimate=pl.CostEstimate(flops=5 * 10**9, bytes_accessed=4 * 10**6, transcendentals=0),
        name="spread_out",
    )


def look_up(pixels, channels, targets, chunk):
    tiles = targets // LANES
    half = pixels // 2

    def kernel(
        place, own_ref, other_ref, right_ref, spread_hbm, pool_ref, motion_ref,
        out_own, out_other, left, rest, vol, looked, looked_low, weight, spread_ref, sem,
    ):
        spread_copy = pltpu.make_async_copy(spread_hbm, spread_ref, sem)
        spread_copy.start()
        scale = channels**-0.5
        first = place[3]
        left[:half, :] = own_ref[:, :channels]
        left[half:, :] = other_ref[:, :channels]
        rest[:half, :] = own_ref[:, channels:]
        rest[half:, :] = other_ref[:, channels:]
        weight[...] = jnp.zeros(weight.shape, F32)
        for level in range(LEVELS):
            weight[level * LANES : level * LANES + AREA, :] = motion_ref[level * AREA : (level + 1) * AREA, :]
        right = right_ref[...]
        contract_last = (((1,), (1,)), ((), ()))
        pooled = jnp.dot(pool_ref[...], right, preferred_element_type=F32)
        high = pooled.astype(BF16)
        low = (pooled - high.astype(F32)).astype(BF16)
        vol[:, :targets] = lax.dot_general(left[...], right, contract_last, preferred_element_type=F32)
        vol[:, targets:] = lax.dot_general(
            left[...], high, contract_last, preferred_element_type=F32
        ) + lax.dot_general(left[...], low, contract_last, preferred_element_type=F32)

        def step(index, carry):
            rows = pl.ds(pl.multiple_of(index * chunk, chunk), chunk)
            shape = (chunk, LANES)
            lane = iota(shape, 1)
            a_of = lane // SIDE
            b_of = lane - a_of * SIDE - RADIUS
            a_of = a_of - RADIUS
            in_window = lane < AREA
            centers = centers_of(place, rest[rows, :].astype(F32), index, chunk)
            for level in range(LEVELS):
                height, apart, width = LANES >> level, 64 >> level, max(4 >> level, 1)
                row = centers[level][0] + a_of
                col = centers[level][1] + b_of - (first >> level)
                within = col & (apart - 1)
                valid = inside(row, height) & inside(col, 2 * apart) & (within < width) & in_window
                strip = ((col >> (6 - level)) & 1) ^ place[4]
                start, count = ((0, tiles), (tiles, 2), (tiles + 2, 1), (tiles + 2, 1))[level]
                if level == 0:
                    cell = target_of(row, strip, within)
                else:
                    cell = (strip * height + row) * width + within + (64 if level == 3 else 0)
                which = jnp.where(valid, cell >> 7, -1)
                found = jnp.zeros(shape, F32)
                for tile in range(count):
                    at = (start + tile) * LANES
                    picked = take(vol[rows, at : at + LANES], cell)
                    found = jnp.where(which == tile, picked, found)
                found = found * scale
                upper = found.astype(BF16)
                looked[rows, level * LANES : (level + 1) * LANES] = upper
                looked_low[rows, level * LANES : (level + 1) * LANES] = (found - upper.astype(F32)).astype(BF16)
            return carry

        lax.fori_loop(0, pixels // chunk, step, 0)

        weight_high = weight[...].astype(BF16)
        weight_low = (weight[...] - weight_high.astype(F32)).astype(BF16)
        motion = jnp.dot(looked[...], weight_high, preferred_element_type=F32)
        motion = motion + jnp.dot(looked[...], weight_low, preferred_element_type=F32)
        motion = motion + jnp.dot(looked_low[...], weight_high, preferred_element_type=F32)
        spread_copy.wait()
        grad_left = jnp.dot(spread_ref[...], right, preferred_element_type=F32) * scale
        out_own[:, :channels] = motion[:half]
        out_own[:, channels:] = grad_left[:half]
        out_other[:, :channels] = motion[half:].astype(BF16)
        out_other[:, channels:] = grad_left[half:].astype(BF16)

    vmem, hbm = pl.BlockSpec(memory_space=pltpu.VMEM), pl.BlockSpec(memory_space=pltpu.HBM)
    return pl.pallas_call(
        kernel,
        out_shape=(
            jax.ShapeDtypeStruct((half, 2 * channels), F32),
            jax.ShapeDtypeStruct((half, 2 * channels), BF16),
        ),
        in_specs=[pl.BlockSpec(memory_space=pltpu.SMEM)] + [vmem] * 3 + [hbm] + [vmem] * 2,
        out_specs=[vmem] * 2,
        scratch_shapes=[
            pltpu.VMEM((pixels, channels), BF16),
            pltpu.VMEM((pixels, LEVELS * AREA + 2), BF16),
            pltpu.VMEM((pixels, targets + 3 * LANES), F32),
            pltpu.VMEM((pixels, LEVELS * LANES), BF16),
            pltpu.VMEM((pixels, LEVELS * LANES), BF16),
            pltpu.VMEM((LEVELS * LANES, channels), F32),
            pltpu.VMEM((pixels, targets), BF16),
            pltpu.SemaphoreType.DMA,
        ],
        compiler_params=pltpu.CompilerParams(vmem_limit_bytes=24 * 2**20),
        cost_estimate=pl.CostEstimate(flops=6 * 10**9, bytes_accessed=4 * 10**6, transcendentals=0),
        name="look_up",
    )


def add_up(parts, cells, channels, hidden_size):
    def kernel(parts_ref, hidden_ref, context_ref, joined_ref, grad_ref):
        total = parts_ref[0].astype(F32)
        for part in range(1, parts):
            total = total + parts_ref[part].astype(F32)
        joined_ref[:, :hidden_size] = hidden_ref[...]
        joined_ref[:, hidden_size : hidden_size + channels] = jnp.maximum(total[:, :channels], 0.0).astype(BF16)
        joined_ref[:, hidden_size + channels :] = context_ref[...]
        grad_ref[...] = total[:, channels:]

    vmem, hbm = pl.BlockSpec(memory_space=pltpu.VMEM), pl.BlockSpec(memory_space=pltpu.HBM)
    return pl.pallas_call(
        kernel,
        out_shape=(
            jax.ShapeDtypeStruct((cells, 2 * channels), BF16),
            jax.ShapeDtypeStruct((cells, channels), F32),
        ),
        in_specs=[vmem] * 3,
        out_specs=[vmem] * 2,
        compiler_params=pltpu.CompilerParams(vmem_limit_bytes=16 * 2**20),
        name="add_up",
    )


def sum_parts(parts, rows, cols, channels):
    def kernel(parts_ref, out_ref):
        total = parts_ref[0].astype(F32)
        for part in range(1, parts):
            total = total + parts_ref[part].astype(F32)
        for row in range(rows):
            out_ref[row] = total[row * cols : (row + 1) * cols]

    vmem = pl.BlockSpec(memory_space=pltpu.VMEM)
    return pl.pallas_call(
        kernel,
        out_shape=jax.ShapeDtypeStruct((rows, cols, channels), F32),
        in_specs=[vmem],
        out_specs=vmem,
        compiler_params=pltpu.CompilerParams(vmem_limit_bytes=16 * 2**20),
        name="sum_parts",
    )


def warm(*weights):
    def kernel(*refs):
        total = refs[0][0, :16, :LANES]
        for ref in refs[1:-1]:
            total = total + ref[0, :16, :LANES]
        refs[-1][...] = total

    vmem = pl.BlockSpec(memory_space=pltpu.VMEM)
    return pl.pallas_call(
        kernel,
        out_shape=jax.ShapeDtypeStruct((16, LANES), BF16),
        in_specs=[vmem] * len(weights),
        out_specs=vmem,
        compiler_params=pltpu.CompilerParams(vmem_limit_bytes=24 * 2**20),
        cost_estimate=pl.CostEstimate(flops=2 * 10**9, bytes_accessed=4 * 10**6, transcendentals=0),
        name="warm",
    )(*weights)


def gru(tile_rows, tile_cols, hidden_size, taps):
    high, wide = tile_rows + 8, tile_cols + 8

    def sigmoid(x):
        return 1.0 / (1.0 + jnp.exp(-x))

    def kernel(cells_ref, rg_ref, rc_ref, cg_ref, cc_ref, warm_ref, out_ref):
        flat = high * wide
        hidden_bf = cells_ref[:, :, :hidden_size].reshape(flat, hidden_size)
        inputs = cells_ref[:, :, hidden_size:].reshape(flat, -1)
        hidden = hidden_bf.astype(F32)

        def conv_x(source, weight_ref):
            total = None
            for tap in range(taps):
                product = jnp.dot(source, weight_ref[tap], preferred_element_type=F32)
                shift = (2 - tap) % flat
                if shift:
                    product = pltpu.roll(product, shift, 0)
                total = product if total is None else total + product
            return total

        gates = sigmoid(conv_x(jnp.concatenate([hidden_bf, inputs], axis=-1), rg_ref))
        update, reset = gates[:, :hidden_size], gates[:, hidden_size:]
        reset_state = (reset * hidden).astype(BF16)
        candidate = jnp.tanh(conv_x(jnp.concatenate([reset_state, inputs], axis=-1), rc_ref))
        middle = (1.0 - update) * hidden + update * candidate

        def own_columns(values):
            moved = pltpu.roll(values, flat - 4, 0).reshape(high, wide, -1)
            return moved[:, :tile_cols].reshape(high * tile_cols, -1)

        middle_bf = own_columns(middle).astype(BF16)
        inputs = own_columns(inputs.astype(F32)).astype(BF16)
        middle = middle_bf.astype(F32)

        def conv_y(source, weight_ref, count):
            total = None
            for tap in range(taps):
                product = jnp.dot(source, weight_ref[tap], preferred_element_type=F32)
                part = product[tap * tile_cols : (tap + count) * tile_cols]
                total = part if total is None else total + part
            return total

        gates = sigmoid(conv_y(jnp.concatenate([middle_bf, inputs], axis=-1), cg_ref, high - 4))
        reset = gates[:, hidden_size:]
        update = gates[2 * tile_cols : (2 + tile_rows) * tile_cols, :hidden_size]
        reset_state = (reset * middle[2 * tile_cols : (high - 2) * tile_cols]).astype(F32)
        edge = jnp.zeros((2 * tile_cols, hidden_size), F32)
        reset_state = jnp.concatenate([edge, reset_state, edge], axis=0).astype(BF16)
        joined = jnp.concatenate([reset_state, inputs], axis=-1)
        total = None
        for tap in range(taps):
            product = jnp.dot(joined, cc_ref[tap], preferred_element_type=F32)
            part = product[(tap + 2) * tile_cols : (tap + 2 + tile_rows) * tile_cols]
            total = part if total is None else total + part
        candidate = jnp.tanh(total)
        center = middle[4 * tile_cols : (4 + tile_rows) * tile_cols]
        out_ref[...] = (1.0 - update) * center + update * candidate

    return pl.pallas_call(
        kernel,
        out_shape=jax.ShapeDtypeStruct((tile_rows * tile_cols, hidden_size), F32),
        in_specs=[pl.BlockSpec(memory_space=pltpu.VMEM)] * 6,
        out_specs=pl.BlockSpec(memory_space=pltpu.VMEM),
        compiler_params=pltpu.CompilerParams(vmem_limit_bytes=24 * 2**20),
        cost_estimate=pl.CostEstimate(flops=10**9, bytes_accessed=5 * 10**6, transcendentals=10**5),
        name="gru",
    )


def with_halo(cells, axis, dim, width):
    count = lax.axis_size(axis)
    ends = count - 1
    head = lax.slice_in_dim(cells, 0, width, axis=dim)
    tail = lax.slice_in_dim(cells, cells.shape[dim] - width, cells.shape[dim], axis=dim)
    return jnp.concatenate(
        [
            lax.ppermute(tail, axis, [(i, (i + 1) % count) for i in range(ends)]),
            cells,
            lax.ppermute(head, axis, [((i + 1) % count, i) for i in range(ends)]),
        ],
        axis=dim,
    )


def swap(block, axis, bit):
    return lax.ppermute(block, axis, [(i, i ^ bit) for i in range(lax.axis_size(axis))])


ROW = ("yh", "z", "core")
COL = ("x", "yl")
SPREAD = ("yh", "x", "yl")


def shards(
    left_features,
    right_features,
    flow_offsets,
    look_cotangent,
    hidden_state,
    context,
    motion_weight,
    row_gates,
    row_candidate,
    column_gates,
    column_candidate,
):
    tile_rows, tile_cols, channels = left_features.shape
    strip_rows, strip_cols = right_features.shape[:2]
    hidden_size = hidden_state.shape[-1]
    zs = lax.axis_size("z")
    cells = tile_rows * tile_cols
    pixels = 2 * zs * cells
    strip = strip_rows * strip_cols
    targets = lax.axis_size(SPREAD) * strip
    first_col = lax.axis_index(COL) * tile_cols

    place = jnp.stack(
        [
            lax.axis_index("yh") * (tile_rows * 2 * zs),
            first_col,
            lax.axis_index("core"),
            lax.axis_index(("z", "core")) * strip_cols,
            lax.axis_index("yh"),
        ]
    ).astype(I32)
    lefts, right = pack(cells, tile_cols, channels, zs)(
        left_features.reshape(cells, channels),
        look_cotangent.reshape(cells, -1),
        flow_offsets,
        right_features,
    )

    left_cot = lax.all_to_all(lefts, "z", 0, 0).reshape(pixels // 2, -1)
    pair = (right, swap(right, "yh", 1))
    rights = jnp.concatenate(
        [jnp.broadcast_to(tile[None], (lax.axis_size(COL),) + tile.shape) for tile in pair], axis=1
    )
    left_cot, rights = lax.optimization_barrier((left_cot, rights))
    left_cot_other = swap(left_cot, "core", 1)
    right = lax.all_to_all(rights, COL, 0, 0).reshape(targets, channels)

    pool = jnp.asarray(pool_matrix(LANES, 2, strip_cols))
    spread, grad = spread_out(pixels, channels, targets, 128, targets // strip)(place, left_cot, left_cot_other, pool)
    outgoing, outgoing_other = look_up(pixels, channels, targets, 128)(
        place, left_cot, left_cot_other, right, spread, pool, motion_weight
    )

    outgoing = (outgoing + swap(outgoing_other, "core", 1).astype(F32)).astype(BF16)
    parts = lax.all_to_all(outgoing.reshape(zs, cells, 2 * channels), "z", 0, 0)
    parts, grad = lax.optimization_barrier((parts, grad))
    grad = lax.all_to_all(grad, SPREAD, 0, 0)
    grad_right = sum_parts(targets // strip, strip_rows, strip_cols, channels)(grad)

    joined, grad_left = add_up(zs, cells, channels, hidden_size)(
        parts, hidden_state.reshape(cells, hidden_size), context.reshape(cells, -1)
    )
    joined = joined.reshape(tile_rows, tile_cols, -1)
    joined = with_halo(with_halo(joined, ROW, 0, 4), COL, 1, 4)
    new_hidden = gru(tile_rows, tile_cols, hidden_size, row_gates.shape[0])(
        joined, row_gates, row_candidate, column_gates, column_candidate,
        warm(row_gates, row_candidate, column_gates, column_candidate),
    )
    return (
        new_hidden.reshape(hidden_state.shape),
        grad_left.reshape(left_features.shape),
        grad_right,
    )


def solution(mesh):
    mesh = jax.sharding.Mesh(mesh.devices.reshape(2, 8, 2, 4, 4), ROW + COL)
    tiled = P(ROW, COL, None)
    in_specs = (tiled, P(COL, ROW, None), P(None, ROW, None), tiled, tiled, tiled) + (P(),) * 5
    out_specs = (tiled, tiled, P(COL, ROW, None))
    return jax.shard_map(shards, mesh=mesh, in_specs=in_specs, out_specs=out_specs, check_vma=False)
```

```python
import jax
import jax.numpy as jnp
import numpy as np
from jax import lax
from jax.experimental import pallas as pl
from jax.experimental.pallas import tpu as pltpu
from jax.sharding import PartitionSpec as P

LEVELS = 4
RADIUS = 4
SIDE = 2 * RADIUS + 1
AREA = SIDE * SIDE
LANES = 128
F32 = jnp.float32
BF16 = jnp.bfloat16
I32 = jnp.int32


def iota(shape, dim):
    return lax.broadcasted_iota(I32, shape, dim)


def target_of(row, strip, col):
    return ((row >> 3) << 6) | (strip << 5) | ((row & 7) << 2) | col


def pool_matrix(rows, strips, width):
    count = np.arange(rows * strips * width)
    strip, row, col = count // (rows * width), count // width % rows, count % width
    target = target_of(row, strip, col)
    parts = []
    for level in (1, 2, 3):
        high, wide = rows >> level, max(width >> level, 1)
        cell = (strip * high + (row >> level)) * wide + (col >> level)
        part = np.zeros((strips * high * wide, count.size), np.float32)
        part[cell, target] = 0.25**level
        parts.append(part)
    pooled = np.concatenate(parts, axis=0)
    padded = -(-pooled.shape[0] // LANES) * LANES
    return np.pad(pooled, ((0, padded - pooled.shape[0]), (0, 0))).astype(BF16)


def take(values, index):
    return jnp.take_along_axis(values, index & (LANES - 1), axis=1, mode="promise_in_bounds")


def inside(index, count):
    return (index >= 0) & (index < count)


def pack(cells, tile_cols, channels, lefts):
    width = channels + LEVELS * AREA + 2

    def kernel(left_ref, cot_ref, flow_ref, right_ref, lefts_hbm, right_out, left, wide, sems):
        first_col = lax.axis_index(COL) * tile_cols
        for row in range(right_ref.shape[0]):
            step = right_ref.shape[1]
            wide[row * step : (row + 1) * step, :] = right_ref[row].astype(F32)
        right_out[...] = wide[...].astype(BF16)
        left[:, :channels] = left_ref[...]
        left[:, channels : width - 2] = cot_ref[...]
        chosen = iota((tile_cols, LANES), 1) == first_col + iota((tile_cols, LANES), 0)
        for axis in range(2):
            columns = []
            for row in range(cells // tile_cols):
                values = jnp.broadcast_to(flow_ref[axis, row : row + 1, :].astype(F32), (tile_cols, LANES))
                columns.append(jnp.sum(jnp.where(chosen, values, 0.0), axis=1, keepdims=True))
            column = jnp.concatenate(columns, axis=0).astype(BF16)
            left[:, width - 2 + axis : width - 1 + axis] = column
        copies = [pltpu.make_async_copy(left, lefts_hbm.at[i], sems.at[i]) for i in range(lefts)]
        for copy in copies:
            copy.start()
        for copy in copies:
            copy.wait()

    vmem, hbm = pl.BlockSpec(memory_space=pltpu.VMEM), pl.BlockSpec(memory_space=pltpu.HBM)
    return pl.pallas_call(
        kernel,
        out_shape=(
            jax.ShapeDtypeStruct((lefts, cells, width), BF16),
            jax.ShapeDtypeStruct((cells, channels), BF16),
        ),
        in_specs=[vmem] * 4,
        out_specs=[hbm, vmem],
        scratch_shapes=[
            pltpu.VMEM((cells, width), BF16),
            pltpu.VMEM((cells, channels), F32),
            pltpu.SemaphoreType.DMA((lefts,)),
        ],
        compiler_params=pltpu.CompilerParams(vmem_limit_bytes=60 * 2**20),
        name="pack",
    )


def centers_of(place, given, index, chunk):
    shape = (chunk, LANES)
    pixel = index * chunk + iota(shape, 0)
    core = place[2] ^ (pixel >> 8)
    row = place[0] + ((pixel >> 5) & 7) * 8 + core * 4 + ((pixel >> 3) & 3)
    col = place[1] + (pixel & 7)
    row = row + jnp.broadcast_to(given[:, LEVELS * AREA : LEVELS * AREA + 1], shape).astype(I32)
    col = col + jnp.broadcast_to(given[:, LEVELS * AREA + 1 : LEVELS * AREA + 2], shape).astype(I32)
    return [(row >> level, col >> level) for level in range(LEVELS)]


def spread_out(pixels, channels, targets, chunk, blocks):
    tiles = targets // LANES
    size = targets // blocks
    half = pixels // 2

    def kernel(
        place, own_ref, other_ref, pool_ref, spread_hbm, grad_hbm,
        left, rest, fine, coarse, spread_ref, grad_ref, sems,
    ):
        scale = channels**-0.5
        first = place[3]
        left[:half, :] = own_ref[:, :channels]
        left[half:, :] = other_ref[:, :channels]
        rest[:half, :] = own_ref[:, channels:]
        rest[half:, :] = other_ref[:, channels:]

        def step(index, carry):
            rows = pl.ds(pl.multiple_of(index * chunk, chunk), chunk)
            shape = (chunk, LANES)
            lane = iota(shape, 1)
            given = rest[rows, :].astype(F32)
            centers = centers_of(place, given, index, chunk)
            cots = []
            for level in range(LEVELS):
                part = given[:, level * AREA : (level + 1) * AREA]
                cots.append(jnp.pad(part, ((0, 0), (0, LANES - AREA))))

            def window(level, row, col):
                a, b = row - centers[level][0], col + (first >> level) - centers[level][1]
                valid = (jnp.abs(a) <= RADIUS) & (jnp.abs(b) <= RADIUS)
                return jnp.where(valid, take(cots[level], a * SIDE + b + AREA // 2), 0.0)

            flip = place[4]
            a = ((lane >> 6) << 3) + ((lane >> 2) & 7) - centers[0][0]
            b = ((((lane >> 5) & 1) ^ flip) << 6) + (lane & 3) + first - centers[0][1]
            near_col = jnp.abs(b) <= RADIUS
            entry = a * SIDE + b + AREA // 2
            for tile in range(tiles):
                valid = near_col & (jnp.abs(a + 16 * tile) <= RADIUS)
                picked = take(cots[0], entry + 16 * SIDE * tile)
                fine[rows, tile * LANES : (tile + 1) * LANES] = jnp.where(valid, picked, 0.0)
            for tile in range(2):
                cell = window(1, lane >> 1, ((tile ^ flip) << 5) + (lane & 1))
                coarse[rows, tile * LANES : (tile + 1) * LANES] = cell.astype(BF16)
            second = window(2, lane & 31, (((lane >> 5) & 1) ^ flip) << 4)
            third = window(3, lane & 15, (((lane >> 4) & 1) ^ flip) << 3)
            cell = jnp.where(lane < 64, second, jnp.where(lane < 96, third, 0.0))
            coarse[rows, 2 * LANES :] = cell.astype(BF16)
            return carry

        lax.fori_loop(0, pixels // chunk, step, 0)

        spread = (fine[...] + jnp.dot(coarse[...], pool_ref[...], preferred_element_type=F32)).astype(BF16)
        spread_ref[...] = spread
        spread_copy = pltpu.make_async_copy(spread_ref, spread_hbm, sems.at[0])
        spread_copy.start()
        grad_ref[...] = (
            lax.dot_general(spread, left[...], (((0,), (0,)), ((), ())), preferred_element_type=F32) * scale
        ).astype(BF16)
        grad_copies = []
        for block in range(blocks):
            owner = ((block & 1) ^ place[4]) * (blocks // 2) + (block >> 1)
            copy = pltpu.make_async_copy(
                grad_ref.at[block * size : (block + 1) * size], grad_hbm.at[owner], sems.at[1 + block]
            )
            copy.start()
            grad_copies.append(copy)
        spread_copy.wait()
        for copy in grad_copies:
            copy.wait()

    vmem, hbm = pl.BlockSpec(memory_space=pltpu.VMEM), pl.BlockSpec(memory_space=pltpu.HBM)
    return pl.pallas_call(
        kernel,
        out_shape=(
            jax.ShapeDtypeStruct((pixels, targets), BF16),
            jax.ShapeDtypeStruct((blocks, size, channels), BF16),
        ),
        in_specs=[pl.BlockSpec(memory_space=pltpu.SMEM)] + [vmem] * 3,
        out_specs=[hbm] * 2,
        scratch_shapes=[
            pltpu.VMEM((pixels, channels), BF16),
            pltpu.VMEM((pixels, LEVELS * AREA + 2), BF16),
            pltpu.VMEM((pixels, targets), F32),
            pltpu.VMEM((pixels, 3 * LANES), BF16),
            pltpu.VMEM((pixels, targets), BF16),
            pltpu.VMEM((targets, channels), BF16),
            pltpu.SemaphoreType.DMA((1 + blocks,)),
        ],
        compiler_params=pltpu.CompilerParams(vmem_limit_bytes=24 * 2**20),
        cost_estimate=pl.CostEstimate(flops=5 * 10**9, bytes_accessed=4 * 10**6, transcendentals=0),
        name="spread_out",
    )


def look_up(pixels, channels, targets, chunk):
    tiles = targets // LANES
    half = pixels // 2

    def kernel(
        place, own_ref, other_ref, right_ref, spread_hbm, pool_ref, motion_ref,
        out_own, out_other, left, rest, vol, looked, looked_low, weight, spread_ref, sem,
    ):
        spread_copy = pltpu.make_async_copy(spread_hbm, spread_ref, sem)
        spread_copy.start()
        scale = channels**-0.5
        first = place[3]
        left[:half, :] = own_ref[:, :channels]
        left[half:, :] = other_ref[:, :channels]
        rest[:half, :] = own_ref[:, channels:]
        rest[half:, :] = other_ref[:, channels:]
        weight[...] = jnp.zeros(weight.shape, F32)
        for level in range(LEVELS):
            weight[level * LANES : level * LANES + AREA, :] = motion_ref[level * AREA : (level + 1) * AREA, :]
        right = right_ref[...]
        contract_last = (((1,), (1,)), ((), ()))
        pooled = jnp.dot(pool_ref[...], right, preferred_element_type=F32)
        high = pooled.astype(BF16)
        low = (pooled - high.astype(F32)).astype(BF16)
        vol[:, :targets] = lax.dot_general(left[...], right, contract_last, preferred_element_type=F32)
        vol[:, targets:] = lax.dot_general(
            left[...], high, contract_last, preferred_element_type=F32
        ) + lax.dot_general(left[...], low, contract_last, preferred_element_type=F32)

        def step(index, carry):
            rows = pl.ds(pl.multiple_of(index * chunk, chunk), chunk)
            shape = (chunk, LANES)
            lane = iota(shape, 1)
            a_of = lane // SIDE
            b_of = lane - a_of * SIDE - RADIUS
            a_of = a_of - RADIUS
            in_window = lane < AREA
            centers = centers_of(place, rest[rows, :].astype(F32), index, chunk)
            for level in range(LEVELS):
                height, apart, width = LANES >> level, 64 >> level, max(4 >> level, 1)
                row = centers[level][0] + a_of
                col = centers[level][1] + b_of - (first >> level)
                within = col & (apart - 1)
                valid = inside(row, height) & inside(col, 2 * apart) & (within < width) & in_window
                strip = ((col >> (6 - level)) & 1) ^ place[4]
                start, count = ((0, tiles), (tiles, 2), (tiles + 2, 1), (tiles + 2, 1))[level]
                if level == 0:
                    cell = target_of(row, strip, within)
                else:
                    cell = (strip * height + row) * width + within + (64 if level == 3 else 0)
                which = jnp.where(valid, cell >> 7, -1)
                found = jnp.zeros(shape, F32)
                for tile in range(count):
                    at = (start + tile) * LANES
                    picked = take(vol[rows, at : at + LANES], cell)
                    found = jnp.where(which == tile, picked, found)
                found = found * scale
                upper = found.astype(BF16)
                looked[rows, level * LANES : (level + 1) * LANES] = upper
                looked_low[rows, level * LANES : (level + 1) * LANES] = (found - upper.astype(F32)).astype(BF16)
            return carry

        lax.fori_loop(0, pixels // chunk, step, 0)

        weight_high = weight[...].astype(BF16)
        weight_low = (weight[...] - weight_high.astype(F32)).astype(BF16)
        motion = jnp.dot(looked[...], weight_high, preferred_element_type=F32)
        motion = motion + jnp.dot(looked[...], weight_low, preferred_element_type=F32)
        motion = motion + jnp.dot(looked_low[...], weight_high, preferred_element_type=F32)
        spread_copy.wait()
        grad_left = jnp.dot(spread_ref[...], right, preferred_element_type=F32) * scale
        out_own[:, :channels] = motion[:half]
        out_own[:, channels:] = grad_left[:half]
        out_other[:, :channels] = motion[half:].astype(BF16)
        out_other[:, channels:] = grad_left[half:].astype(BF16)

    vmem, hbm = pl.BlockSpec(memory_space=pltpu.VMEM), pl.BlockSpec(memory_space=pltpu.HBM)
    return pl.pallas_call(
        kernel,
        out_shape=(
            jax.ShapeDtypeStruct((half, 2 * channels), F32),
            jax.ShapeDtypeStruct((half, 2 * channels), BF16),
        ),
        in_specs=[pl.BlockSpec(memory_space=pltpu.SMEM)] + [vmem] * 3 + [hbm] + [vmem] * 2,
        out_specs=[vmem] * 2,
        scratch_shapes=[
            pltpu.VMEM((pixels, channels), BF16),
            pltpu.VMEM((pixels, LEVELS * AREA + 2), BF16),
            pltpu.VMEM((pixels, targets + 3 * LANES), F32),
            pltpu.VMEM((pixels, LEVELS * LANES), BF16),
            pltpu.VMEM((pixels, LEVELS * LANES), BF16),
            pltpu.VMEM((LEVELS * LANES, channels), F32),
            pltpu.VMEM((pixels, targets), BF16),
            pltpu.SemaphoreType.DMA,
        ],
        compiler_params=pltpu.CompilerParams(vmem_limit_bytes=24 * 2**20),
        cost_estimate=pl.CostEstimate(flops=6 * 10**9, bytes_accessed=4 * 10**6, transcendentals=0),
        name="look_up",
    )


def add_up(parts, cells, channels, hidden_size):
    def kernel(parts_ref, hidden_ref, context_ref, joined_ref, grad_ref):
        total = parts_ref[0].astype(F32)
        for part in range(1, parts):
            total = total + parts_ref[part].astype(F32)
        joined_ref[:, :hidden_size] = hidden_ref[...]
        joined_ref[:, hidden_size : hidden_size + channels] = jnp.maximum(total[:, :channels], 0.0).astype(BF16)
        joined_ref[:, hidden_size + channels :] = context_ref[...]
        grad_ref[...] = total[:, channels:]

    vmem, hbm = pl.BlockSpec(memory_space=pltpu.VMEM), pl.BlockSpec(memory_space=pltpu.HBM)
    return pl.pallas_call(
        kernel,
        out_shape=(
            jax.ShapeDtypeStruct((cells, 2 * channels), BF16),
            jax.ShapeDtypeStruct((cells, channels), F32),
        ),
        in_specs=[vmem] * 3,
        out_specs=[vmem] * 2,
        compiler_params=pltpu.CompilerParams(vmem_limit_bytes=16 * 2**20),
        name="add_up",
    )


def sum_parts(parts, rows, cols, channels):
    def kernel(parts_ref, out_ref):
        total = parts_ref[0].astype(F32)
        for part in range(1, parts):
            total = total + parts_ref[part].astype(F32)
        for row in range(rows):
            out_ref[row] = total[row * cols : (row + 1) * cols]

    vmem = pl.BlockSpec(memory_space=pltpu.VMEM)
    return pl.pallas_call(
        kernel,
        out_shape=jax.ShapeDtypeStruct((rows, cols, channels), F32),
        in_specs=[vmem],
        out_specs=vmem,
        compiler_params=pltpu.CompilerParams(vmem_limit_bytes=16 * 2**20),
        name="sum_parts",
    )


def warm(*weights):
    def kernel(*refs):
        total = refs[0][0, :16, :LANES]
        for ref in refs[1:-1]:
            total = total + ref[0, :16, :LANES]
        refs[-1][...] = total

    vmem = pl.BlockSpec(memory_space=pltpu.VMEM)
    return pl.pallas_call(
        kernel,
        out_shape=jax.ShapeDtypeStruct((16, LANES), BF16),
        in_specs=[vmem] * len(weights),
        out_specs=vmem,
        compiler_params=pltpu.CompilerParams(vmem_limit_bytes=24 * 2**20),
        cost_estimate=pl.CostEstimate(flops=2 * 10**9, bytes_accessed=4 * 10**6, transcendentals=0),
        name="warm",
    )(*weights)


def gru(tile_rows, tile_cols, hidden_size, taps):
    high, wide = tile_rows + 8, tile_cols + 8

    def sigmoid(x):
        return 1.0 / (1.0 + jnp.exp(-x))

    def kernel(cells_ref, rg_ref, rc_ref, cg_ref, cc_ref, warm_ref, out_ref):
        flat = high * wide
        hidden_bf = cells_ref[:, :, :hidden_size].reshape(flat, hidden_size)
        inputs = cells_ref[:, :, hidden_size:].reshape(flat, -1)
        hidden = hidden_bf.astype(F32)

        def conv_x(source, weight_ref):
            total = None
            for tap in range(taps):
                product = jnp.dot(source, weight_ref[tap], preferred_element_type=F32)
                shift = (2 - tap) % flat
                if shift:
                    product = pltpu.roll(product, shift, 0)
                total = product if total is None else total + product
            return total

        gates = sigmoid(conv_x(jnp.concatenate([hidden_bf, inputs], axis=-1), rg_ref))
        update, reset = gates[:, :hidden_size], gates[:, hidden_size:]
        reset_state = (reset * hidden).astype(BF16)
        candidate = jnp.tanh(conv_x(jnp.concatenate([reset_state, inputs], axis=-1), rc_ref))
        middle = (1.0 - update) * hidden + update * candidate

        def own_columns(values):
            moved = pltpu.roll(values, flat - 4, 0).reshape(high, wide, -1)
            return moved[:, :tile_cols].reshape(high * tile_cols, -1)

        middle_bf = own_columns(middle).astype(BF16)
        inputs = own_columns(inputs.astype(F32)).astype(BF16)
        middle = middle_bf.astype(F32)

        def conv_y(source, weight_ref, count):
            total = None
            for tap in range(taps):
                product = jnp.dot(source, weight_ref[tap], preferred_element_type=F32)
                part = product[tap * tile_cols : (tap + count) * tile_cols]
                total = part if total is None else total + part
            return total

        gates = sigmoid(conv_y(jnp.concatenate([middle_bf, inputs], axis=-1), cg_ref, high - 4))
        reset = gates[:, hidden_size:]
        update = gates[2 * tile_cols : (2 + tile_rows) * tile_cols, :hidden_size]
        reset_state = (reset * middle[2 * tile_cols : (high - 2) * tile_cols]).astype(F32)
        edge = jnp.zeros((2 * tile_cols, hidden_size), F32)
        reset_state = jnp.concatenate([edge, reset_state, edge], axis=0).astype(BF16)
        joined = jnp.concatenate([reset_state, inputs], axis=-1)
        total = None
        for tap in range(taps):
            product = jnp.dot(joined, cc_ref[tap], preferred_element_type=F32)
            part = product[(tap + 2) * tile_cols : (tap + 2 + tile_rows) * tile_cols]
            total = part if total is None else total + part
        candidate = jnp.tanh(total)
        center = middle[4 * tile_cols : (4 + tile_rows) * tile_cols]
        out_ref[...] = (1.0 - update) * center + update * candidate

    return pl.pallas_call(
        kernel,
        out_shape=jax.ShapeDtypeStruct((tile_rows * tile_cols, hidden_size), F32),
        in_specs=[pl.BlockSpec(memory_space=pltpu.VMEM)] * 6,
        out_specs=pl.BlockSpec(memory_space=pltpu.VMEM),
        compiler_params=pltpu.CompilerParams(vmem_limit_bytes=24 * 2**20),
        cost_estimate=pl.CostEstimate(flops=10**9, bytes_accessed=5 * 10**6, transcendentals=10**5),
        name="gru",
    )


def with_halo(cells, axis, dim, width):
    count = lax.axis_size(axis)
    ends = count - 1
    head = lax.slice_in_dim(cells, 0, width, axis=dim)
    tail = lax.slice_in_dim(cells, cells.shape[dim] - width, cells.shape[dim], axis=dim)
    return jnp.concatenate(
        [
            lax.ppermute(tail, axis, [(i, (i + 1) % count) for i in range(ends)]),
            cells,
            lax.ppermute(head, axis, [((i + 1) % count, i) for i in range(ends)]),
        ],
        axis=dim,
    )


def swap(block, axis, bit):
    return lax.ppermute(block, axis, [(i, i ^ bit) for i in range(lax.axis_size(axis))])


ROW = ("yh", "z", "core")
COL = ("x", "yl")
SPREAD = ("yh", "x", "yl")


def shards(
    left_features,
    right_features,
    flow_offsets,
    look_cotangent,
    hidden_state,
    context,
    motion_weight,
    row_gates,
    row_candidate,
    column_gates,
    column_candidate,
):
    tile_rows, tile_cols, channels = left_features.shape
    strip_rows, strip_cols = right_features.shape[:2]
    hidden_size = hidden_state.shape[-1]
    zs = lax.axis_size("z")
    cells = tile_rows * tile_cols
    pixels = 2 * zs * cells
    strip = strip_rows * strip_cols
    targets = lax.axis_size(SPREAD) * strip
    first_col = lax.axis_index(COL) * tile_cols

    place = jnp.stack(
        [
            lax.axis_index("yh") * (tile_rows * 2 * zs),
            first_col,
            lax.axis_index("core"),
            lax.axis_index(("z", "core")) * strip_cols,
            lax.axis_index("yh"),
        ]
    ).astype(I32)
    lefts, right = pack(cells, tile_cols, channels, zs)(
        left_features.reshape(cells, channels),
        look_cotangent.reshape(cells, -1),
        flow_offsets,
        right_features,
    )

    left_cot = lax.all_to_all(lefts, "z", 0, 0).reshape(pixels // 2, -1)
    pair = (right, swap(right, "yh", 1))
    rights = jnp.concatenate(
        [jnp.broadcast_to(tile[None], (lax.axis_size(COL),) + tile.shape) for tile in pair], axis=1
    )
    left_cot, rights = lax.optimization_barrier((left_cot, rights))
    left_cot_other = swap(left_cot, "core", 1)
    right = lax.all_to_all(rights, COL, 0, 0).reshape(targets, channels)

    pool = jnp.asarray(pool_matrix(LANES, 2, strip_cols))
    spread, grad = spread_out(pixels, channels, targets, 256, targets // strip)(place, left_cot, left_cot_other, pool)
    outgoing, outgoing_other = look_up(pixels, channels, targets, 256)(
        place, left_cot, left_cot_other, right, spread, pool, motion_weight
    )

    outgoing = (outgoing + swap(outgoing_other, "core", 1).astype(F32)).astype(BF16)
    parts = lax.all_to_all(outgoing.reshape(zs, cells, 2 * channels), "z", 0, 0)
    parts, grad = lax.optimization_barrier((parts, grad))
    grad = lax.all_to_all(grad, SPREAD, 0, 0)
    grad_right = sum_parts(targets // strip, strip_rows, strip_cols, channels)(grad)

    joined, grad_left = add_up(zs, cells, channels, hidden_size)(
        parts, hidden_state.reshape(cells, hidden_size), context.reshape(cells, -1)
    )
    joined = joined.reshape(tile_rows, tile_cols, -1)
    joined = with_halo(with_halo(joined, ROW, 0, 4), COL, 1, 4)
    new_hidden = gru(tile_rows, tile_cols, hidden_size, row_gates.shape[0])(
        joined, row_gates, row_candidate, column_gates, column_candidate,
        warm(row_gates, row_candidate, column_gates, column_candidate),
    )
    return (
        new_hidden.reshape(hidden_state.shape),
        grad_left.reshape(left_features.shape),
        grad_right,
    )


def solution(mesh):
    mesh = jax.sharding.Mesh(mesh.devices.reshape(2, 8, 2, 4, 4), ROW + COL)
    tiled = P(ROW, COL, None)
    in_specs = (tiled, P(COL, ROW, None), P(None, ROW, None), tiled, tiled, tiled) + (P(),) * 5
    out_specs = (tiled, tiled, P(COL, ROW, None))
    return jax.shard_map(shards, mesh=mesh, in_specs=in_specs, out_specs=out_specs, check_vma=False)
```
